128 devices in a mesh: seq: 4 (over z_hi, core), vocab: 32 (over y, x, z_lo).
Axes of the slice: x: 4, y: 4, z: 4 (z_hi: 2, z_lo: 2; z = z_hi * 2 + z_lo), core: 2. Of those that a mesh axis runs over, the one named last changes fastest.
Arguments:
- hidden: bfloat16 [256, 8192], P('seq', 'vocab'), may hold values from -80 to 80
- base_logits: float32 [256, 77824], P('seq', 'vocab'), may hold values from -20 to 220
- doc_ids: int32 [256], replicated, may hold values from 0 to 31, never falling along the last dimension, each value on 1 to 64 neighbouring positions
- offsets: int32 [2], replicated, may hold values from 1 to 4, as said below
- block_weight: bfloat16 [2, 8192, 8192], P(None, None, ('seq', 'vocab')), may hold values from -0.0625 to 0.0625
- block_bias: float32 [2, 8192], P(None, ('seq', 'vocab')), may hold values from -6 to 6
- projection: bfloat16 [8192, 77824], P(None, ('vocab', 'seq')), may hold values from -0.19824219 to 0.19824219
Outputs:
- grad_proj: bfloat16 [8192, 77824], P(None, ('vocab', 'seq'))
- grad_block: bfloat16 [2, 8192, 8192], P(None, None, ('seq', 'vocab'))
- grad_bias: float32 [2, 8192], P(None, ('seq', 'vocab'))
- loss: float32 [], replicated
The draws below stay inside these ranges and needn't reach their ends.
Inputs may be any that keep to these rules, and one draw needn't show every extreme that they name: `offsets`: in every draw some head has offset 4.
All inputs are finite; a program needn't handle non-finite values.
Results may differ from the reference program's by a relative error of at most 0.019.
Values may be sent and summed in bfloat16 or wider, within the bound.
No kernel may reach another device: no remote copies, remote signals or barrier semaphores. Data moves between devices by JAX's collectives and lax.ppermute only.
A program may use at most 192 MiB of HBM per device.

```python
import math
import jax
import jax.numpy as jnp
import numpy as np
from jax import lax

D = 8192
VOCAB = 77824
HEADS = 2
WINDOW = 256


def draw_hidden(key, part):
    key = jax.random.fold_in(key, 11)
    first = jax.random.fold_in(key, 0)
    values = jnp.clip(jax.random.normal(first, (WINDOW, D), jnp.float32), -6.0, 6.0)
    return values.astype(jnp.bfloat16)


def draw_base_logits(key, part):
    key = jax.random.fold_in(key, 23)
    first = jax.random.fold_in(key, 0)
    values = jnp.clip(3.0 * jax.random.normal(first, (WINDOW, VOCAB), jnp.float32), -18.0, 18.0)
    return values


def draw_offsets(key, part):
    key = jax.random.fold_in(key, 37)
    first, second = jax.random.split(key)
    values = jax.random.randint(first, (HEADS,), 1, 5)
    chosen = jax.random.randint(second, (), 0, HEADS)
    return jnp.where(jnp.arange(HEADS, dtype=jnp.int32) == chosen, 4, values).astype(jnp.int32)


def block_scale(own_key, extent, cuts, least, top_value):
    def one(position, blocks):
        heights = jax.random.uniform(jax.random.fold_in(jax.random.fold_in(own_key, 6), position), (blocks,), jnp.float32, least / len(cuts), top_value / len(cuts))
        return jnp.repeat(jnp.exp(heights), extent[position] // blocks).reshape((-1,) + (1,) * (len(extent) - position - 1))

    gain = one(*cuts[0])
    for cut in cuts[1:]:
        gain = gain * one(*cut)
    return gain


def length_profile(count, total, limit, skew):
    weights = [(1 << 20) // math.isqrt(standing ** skew) + 1 for standing in range(2, count + 1)]
    spare, counts = total - limit - (count - 1), [1] * (count - 1)
    while spare > 0:
        candidates = [i for i in range(count - 1) if counts[i] < limit]
        mass, remaining = sum([weights[i] for i in candidates]), spare
        for i in candidates:
            more = min(limit - counts[i], max(1, remaining * weights[i] // mass), spare)
            counts[i] = counts[i] + more
            spare = spare - more
    return np.array([limit] + counts)


def ragged(stream_key, amount, total, most, skew):
    if amount == 2:
        one = jax.random.randint(stream_key, (), max(1, total - most), min(most, total - 1) + 1)
        return jnp.stack([one, total - one])
    tallies = jnp.asarray(length_profile(amount, total, most, skew), jnp.int32)
    twos = (amount - 1) // 2
    giver, sink = tallies[1:1 + 2 * twos:2], tallies[2:2 + 2 * twos:2]
    margin = jnp.minimum(giver - 1, most - sink)
    moved = jax.random.randint(jax.random.fold_in(stream_key, 1), (twos,), 0, 1 << 20) % (margin + 1)
    tallies = tallies.at[1:1 + 2 * twos:2].set(giver - moved).at[2:2 + 2 * twos:2].set(sink + moved)
    return tallies[jax.random.permutation(jax.random.fold_in(stream_key, 2), amount)]


def noise(own_key, dims, deviation, bound, pieces=(), kind=jnp.bfloat16):
    drawn = deviation * jax.random.normal(own_key, dims, jnp.float32)
    if pieces:
        drawn = drawn * block_scale(own_key, dims, pieces, -0.22, 0.18)
    return jnp.clip(drawn, -bound, bound).astype(kind)


def setup_inputs(seed: int = 0) -> dict:
    key_of = jax.random.split(jax.random.key(seed), 8)
    hidden = draw_hidden(jax.random.fold_in(key_of[7], 71), 0)
    base_logits = draw_base_logits(jax.random.fold_in(key_of[7], 71), 0)
    doc_ids = jnp.searchsorted(jnp.cumsum(ragged(key_of[2], WINDOW // 8, WINDOW, WINDOW // 4, 2)), jnp.arange(WINDOW), side="right").astype(jnp.int32)
    offsets = draw_offsets(jax.random.fold_in(key_of[7], 71), 0)
    block_weight = noise(key_of[4], (HEADS, D, D), D ** -0.5, 0.0625, ((2, 128),))
    block_bias = noise(key_of[5], (HEADS, D), 1.0, 6.0, ((1, 128),), jnp.float32)
    projection = noise(key_of[6], (D, VOCAB), (3 * D ** -0.5), 0.19824219, ((1, 128),))
    return {"hidden": hidden, "base_logits": base_logits, "doc_ids": doc_ids, "offsets": offsets, "block_weight": block_weight, "block_bias": block_bias, "projection": projection}


def silu_slope(pre_act):
    sigma = jax.nn.sigmoid(pre_act)
    return sigma * (1.0 + pre_act * (1.0 - sigma))


def reference(hidden, base_logits, doc_ids, offsets, block_weight, block_bias, projection):
    window = hidden.shape[0]
    padded = jnp.concatenate([base_logits, jnp.zeros((4, base_logits.shape[1]), jnp.float32)], 0)
    padded_ids = jnp.concatenate([doc_ids, jnp.full((4,), -1, jnp.int32)], 0)
    grad_proj = jnp.zeros(projection.shape, jnp.float32)
    grad_blocks = []
    grad_biases = []
    total_kl = jnp.zeros((), jnp.float32)
    total_count = jnp.zeros((), jnp.float32)
    for head_index in range(HEADS):
        pre_act = jnp.dot(hidden, block_weight[head_index], preferred_element_type=jnp.float32) + block_bias[head_index]
        states = (hidden.astype(jnp.float32) + jax.nn.silu(pre_act)).astype(jnp.bfloat16)
        logits = jnp.dot(states, projection, preferred_element_type=jnp.float32)
        shift = offsets[head_index].astype(jnp.int32)
        target = lax.dynamic_slice_in_dim(padded, shift, window, 0)
        valid = (lax.dynamic_slice_in_dim(padded_ids, shift, window, 0) == doc_ids).astype(jnp.float32)
        log_head = jax.nn.log_softmax(logits, axis=-1)
        log_base = jax.nn.log_softmax(target, axis=-1)
        prob_base = jnp.exp(log_base)
        kl_rows = jnp.sum(prob_base * (log_base - log_head), axis=-1)
        total_kl = total_kl + jnp.sum(valid * kl_rows)
        total_count = total_count + jnp.sum(valid)
        logit_grad = (valid[:, None] * (jnp.exp(log_head) - prob_base)).astype(jnp.bfloat16)
        grad_proj = grad_proj + jnp.dot(states.T, logit_grad, preferred_element_type=jnp.float32)
        state_grad = jnp.dot(logit_grad, projection.T, preferred_element_type=jnp.float32)
        pre_grad = state_grad * silu_slope(pre_act)
        grad_blocks.append(jnp.dot(hidden.T, pre_grad.astype(jnp.bfloat16), preferred_element_type=jnp.float32).astype(jnp.bfloat16))
        grad_biases.append(jnp.sum(pre_grad, axis=0))
    loss = total_kl / jnp.maximum(total_count, 1.0)
    return grad_proj.astype(jnp.bfloat16), jnp.stack(grad_blocks), jnp.stack(grad_biases), loss
```

```python
import functools

import jax
import jax.numpy as jnp
from jax import lax
from jax.experimental import pallas as pl
from jax.experimental.pallas import tpu as pltpu
from jax.sharding import Mesh, PartitionSpec as P

AXES = ("zh", "core", "y", "x", "zl")
CHIPS = ("zh", "y", "x", "zl")
SEQ = ("zh", "core")
VOCAB = ("y", "x", "zl")
BF16 = jnp.bfloat16
F32 = jnp.float32
VMEM_LIMIT = 48 * 1024 * 1024


def swap_core(x):
    return lax.ppermute(x, "core", [(0, 1), (1, 0)])


def gather_chips(x):
    return lax.all_to_all(
        jnp.broadcast_to(x[None], (64,) + x.shape), CHIPS, split_axis=0, concat_axis=0, tiled=True
    )


def params():
    return pltpu.CompilerParams(vmem_limit_bytes=VMEM_LIMIT)


def hidden_block(own_ref, other_ref, index):
    return jnp.concatenate(
        [own_ref[0, index], own_ref[1, index], other_ref[0, index], other_ref[1, index]], axis=0
    )


def states_kernel(place_ref, own_ref, other_ref, weight_ref, bias_ref, pick_ref, pre_ref, packed_ref, cols_ref):
    step = pl.program_id(0)
    per_step = own_ref.shape[1]
    width = own_ref.shape[3]
    cols = packed_ref.shape[0]

    @pl.when(step == 0)
    def _():
        pre_ref[...] = jnp.zeros_like(pre_ref)

    total = pre_ref[...]
    for index in range(per_step):
        block = hidden_block(own_ref, other_ref, index)
        part = weight_ref[:, index * width : (index + 1) * width]
        total += lax.dot_general(part, block, (((1,), (1,)), ((), ())), preferred_element_type=F32)

        @pl.when(step * per_step + index == place_ref[0])
        def _():
            lane = lax.broadcasted_iota(jnp.int32, (cols, width), 1)
            row = lax.broadcasted_iota(jnp.int32, (cols, width), 0)
            select = (lane == row + place_ref[1] * cols).astype(BF16)
            cols_ref[...] = lax.dot_general(
                select, block, (((1,), (1,)), ((), ())), preferred_element_type=F32
            )

    pre_ref[...] = total

    @pl.when(step == pl.num_programs(0) - 1)
    def _():
        pre = total + bias_ref[...]
        pre_ref[...] = pre
        packed = jnp.zeros(packed_ref.shape, F32)
        for head in range(pick_ref.shape[0]):
            own = pre[head * cols : (head + 1) * cols]
            state = (cols_ref[...] + own / (1.0 + jnp.exp(-own))).astype(BF16)
            packed += jnp.dot(state, pick_ref[head], preferred_element_type=F32)
        packed_ref[...] = packed.astype(BF16)


def packed_states(place, own, other, weight, bias, pick, per_step=4):
    _, blocks, rows, width = own.shape
    heads, window, size = pick.shape
    cols = weight.shape[0] // heads
    hidden_spec = pl.BlockSpec((2, per_step, rows, width), lambda i, p: (0, i, 0, 0))
    return pl.pallas_call(
        states_kernel,
        grid_spec=pltpu.PrefetchScalarGridSpec(
            num_scalar_prefetch=1,
            grid=(blocks // per_step,),
            in_specs=[
                hidden_spec,
                hidden_spec,
                pl.BlockSpec((heads * cols, per_step * width), lambda i, p: (0, i)),
                pl.BlockSpec((heads * cols, 1), lambda i, p: (0, 0)),
                pl.BlockSpec((heads, window, size), lambda i, p: (0, 0, 0)),
            ],
            out_specs=[
                pl.BlockSpec((heads * cols, window), lambda i, p: (0, 0)),
                pl.BlockSpec((cols, size), lambda i, p: (0, 0)),
            ],
            scratch_shapes=[pltpu.VMEM((cols, window), F32)],
        ),
        out_shape=[
            jax.ShapeDtypeStruct((heads * cols, window), F32),
            jax.ShapeDtypeStruct((cols, size), BF16),
        ],
        compiler_params=params(),
        name="packed_states",
    )(place, own, other, weight, bias, pick)


def logits_kernel(core_ref, proj_ref, own_ref, other_ref, target_ref, logits_ref, stats_ref):
    step = pl.program_id(0)
    half = pl.num_programs(0) // 2

    @pl.when(step == 0)
    def _():
        logits_ref[...] = jnp.dot(proj_ref[...], own_ref[...], preferred_element_type=F32)

    @pl.when(jnp.logical_and(step > 0, step < half))
    def _():
        logits_ref[...] += jnp.dot(proj_ref[...], own_ref[...], preferred_element_type=F32)

    @pl.when(step >= half)
    def _():
        logits_ref[...] += jnp.dot(proj_ref[...], other_ref[...], preferred_element_type=F32)

    @pl.when(step == pl.num_programs(0) - 1)
    def _():
        logits = logits_ref[...]
        target = target_ref[...]
        top_head = jnp.max(logits, axis=0, keepdims=True)
        top_base = jnp.max(target, axis=0, keepdims=True)
        exp_base = jnp.exp(target - top_base)
        sum_head = jnp.sum(jnp.exp(logits - top_head), axis=0, keepdims=True)
        sum_base = jnp.sum(exp_base, axis=0, keepdims=True)
        cross = jnp.sum(exp_base * (target - logits), axis=0, keepdims=True)
        stats_ref[...] = jnp.concatenate(
            [top_head, sum_head, top_base, sum_base, cross, jnp.zeros((3, cross.shape[1]), F32)], 0
        )


def stretch_logits(core, proj, own, other, target, block=1024):
    stretch, depth = proj.shape
    size = own.shape[1]
    per = depth // 4 // block
    steps = depth // block
    half = steps // 2

    def proj_index(i, c):
        mine = i // half
        j = i % half
        which = jnp.where(mine == 0, c[0], 1 - c[0])
        return (0, ((j // per) * 2 + which) * per + j % per)

    return pl.pallas_call(
        logits_kernel,
        grid_spec=pltpu.PrefetchScalarGridSpec(
            num_scalar_prefetch=1,
            grid=(steps,),
            in_specs=[
                pl.BlockSpec((stretch, block), proj_index),
                pl.BlockSpec((block, size), lambda i, c: (jnp.minimum(i, half - 1), 0)),
                pl.BlockSpec((block, size), lambda i, c: (jnp.maximum(i - half, 0), 0)),
                pl.BlockSpec((stretch, size), lambda i, c: (0, 0)),
            ],
            out_specs=[
                pl.BlockSpec((stretch, size), lambda i, c: (0, 0)),
                pl.BlockSpec((8, size), lambda i, c: (0, 0)),
            ],
        ),
        out_shape=[
            jax.ShapeDtypeStruct((stretch, size), F32),
            jax.ShapeDtypeStruct((8, size), F32),
        ],
        compiler_params=params(),
        name="stretch_logits",
    )(core, proj, own, other, target)


def state_grad_kernel(core_ref, proj_ref, grad_ref, out_ref):
    out_ref[...] = lax.dot_general(
        proj_ref[...], grad_ref[...], (((0,), (0,)), ((), ())), preferred_element_type=F32
    ).astype(BF16)


def state_grad_add_kernel(core_ref, proj_ref, grad_ref, add_ref, out_ref):
    out_ref[...] = (
        lax.dot_general(
            proj_ref[...], grad_ref[...], (((0,), (0,)), ((), ())), preferred_element_type=F32
        )
        + add_ref[...].astype(F32)
    ).astype(BF16)


def state_grad_half(core, proj, grad, add=None, block=1024):
    stretch, depth = proj.shape
    size = grad.shape[1]
    per = depth // 4 // block
    specs = [
        pl.BlockSpec((stretch, block), lambda i, c: (0, ((i // per) * 2 + c[0]) * per + i % per)),
        pl.BlockSpec((stretch, size), lambda i, c: (0, 0)),
    ]
    args = [proj, grad]
    if add is not None:
        specs.append(pl.BlockSpec((block, size), lambda i, c: (i, 0)))
        args.append(add)
    return pl.pallas_call(
        state_grad_kernel if add is None else state_grad_add_kernel,
        grid_spec=pltpu.PrefetchScalarGridSpec(
            num_scalar_prefetch=1,
            grid=(depth // 2 // block,),
            in_specs=specs,
            out_specs=pl.BlockSpec((block, size), lambda i, c: (i, 0)),
        ),
        out_shape=jax.ShapeDtypeStruct((depth // 2, size), BF16),
        compiler_params=params(),
        cost_estimate=pl.CostEstimate(
            flops=stretch * depth * size, bytes_accessed=depth * (stretch + size), transcendentals=0
        ),
        name="state_grad_half",
    )(core, *args)


def grad_proj_kernel(core_ref, grad_ref, own_ref, other_ref, out_ref):
    step = pl.program_id(0)
    half = pl.num_programs(0) // 2

    @pl.when(step < half)
    def _():
        out_ref[...] = lax.dot_general(
            grad_ref[...], own_ref[...], (((1,), (1,)), ((), ())), preferred_element_type=F32
        ).astype(BF16)

    @pl.when(step >= half)
    def _():
        out_ref[...] = lax.dot_general(
            grad_ref[...], other_ref[...], (((1,), (1,)), ((), ())), preferred_element_type=F32
        ).astype(BF16)


def projection_grad(core, grad, own, other, block=1024):
    stretch, size = grad.shape
    depth = own.shape[0] * 2
    per = depth // 4 // block
    steps = depth // block
    half = steps // 2

    def out_index(i, c):
        mine = i // half
        j = i % half
        which = jnp.where(mine == 0, c[0], 1 - c[0])
        return (0, ((j // per) * 2 + which) * per + j % per)

    return pl.pallas_call(
        grad_proj_kernel,
        grid_spec=pltpu.PrefetchScalarGridSpec(
            num_scalar_prefetch=1,
            grid=(steps,),
            in_specs=[
                pl.BlockSpec((stretch, size), lambda i, c: (0, 0)),
                pl.BlockSpec((block, size), lambda i, c: (jnp.minimum(i, half - 1), 0)),
                pl.BlockSpec((block, size), lambda i, c: (jnp.maximum(i - half, 0), 0)),
            ],
            out_specs=pl.BlockSpec((stretch, block), out_index),
        ),
        out_shape=jax.ShapeDtypeStruct((stretch, depth), BF16),
        compiler_params=params(),
        cost_estimate=pl.CostEstimate(
            flops=2 * stretch * depth * size, bytes_accessed=2 * depth * (stretch + size), transcendentals=0
        ),
        name="projection_grad",
    )(core, grad, own, other)


def grad_block_kernel(state_grad_ref, pick_ref, pre_ref, own_ref, other_ref, out_ref, bias_ref, pre_grad_ref):
    step = pl.program_id(0)
    per_step = own_ref.shape[1]
    width = own_ref.shape[3]
    cols = state_grad_ref.shape[0]

    @pl.when(step == 0)
    def _():
        high = state_grad_ref[...].astype(BF16)
        rest = state_grad_ref[...] - high.astype(F32)
        middle = rest.astype(BF16)
        low = (rest - middle.astype(F32)).astype(BF16)
        for head in range(pick_ref.shape[0]):
            own = slice(head * cols, (head + 1) * cols)
            spread = sum(
                lax.dot_general(
                    piece, pick_ref[head], (((1,), (1,)), ((), ())), preferred_element_type=F32
                )
                for piece in (low, middle, high)
            )
            pre = pre_ref[own]
            sigma = 1.0 / (1.0 + jnp.exp(-pre))
            pre_grad = spread * (sigma * (1.0 + pre * (1.0 - sigma)))
            bias_ref[own] = jnp.sum(pre_grad, axis=1, keepdims=True)
            pre_grad_ref[own] = pre_grad.astype(BF16)

    for index in range(per_step):
        block = hidden_block(own_ref, other_ref, index)
        out_ref[:, index * width : (index + 1) * width] = jnp.dot(
            pre_grad_ref[...], block, preferred_element_type=F32
        ).astype(BF16)


def block_grad(state_grad, pick, pre, own, other, per_step=4):
    _, blocks, rows, width = own.shape
    heads, window, size = pick.shape
    cols = state_grad.shape[0]
    hidden_spec = pl.BlockSpec((2, per_step, rows, width), lambda i: (0, i, 0, 0))
    return pl.pallas_call(
        grad_block_kernel,
        grid=(blocks // per_step,),
        in_specs=[
            pl.BlockSpec((cols, size), lambda i: (0, 0)),
            pl.BlockSpec((heads, window, size), lambda i: (0, 0, 0)),
            pl.BlockSpec((heads * cols, window), lambda i: (0, 0)),
            hidden_spec,
            hidden_spec,
        ],
        out_specs=[
            pl.BlockSpec((heads * cols, per_step * width), lambda i: (0, i)),
            pl.BlockSpec((heads * cols, 1), lambda i: (0, 0)),
        ],
        out_shape=[
            jax.ShapeDtypeStruct((heads * cols, blocks * width), BF16),
            jax.ShapeDtypeStruct((heads * cols, 1), F32),
        ],
        scratch_shapes=[pltpu.VMEM((heads * cols, window), BF16)],
        compiler_params=params(),
        name="block_grad",
    )(state_grad, pick, pre, own, other)


def merge(parts):
    top_head = functools.reduce(jnp.maximum, [p[0] for p in parts])
    top_base = functools.reduce(jnp.maximum, [p[2] for p in parts])
    scale_head = [jnp.exp(p[0] - top_head) for p in parts]
    scale_base = [jnp.exp(p[2] - top_base) for p in parts]
    sum_head = sum(p[1] * s for p, s in zip(parts, scale_head))
    sum_base = sum(p[3] * s for p, s in zip(parts, scale_base))
    cross = sum(p[4] * s for p, s in zip(parts, scale_base))
    zero = jnp.zeros_like(cross)
    return jnp.stack([top_head, sum_head, top_base, sum_base, cross, zero, zero, zero])


def merge_all(stats):
    stats = merge([stats, swap_core(stats)])
    for axis in ("x", "y", ("zh", "zl")):
        others = [
            lax.ppermute(stats, axis, [(i, (i + shift) % 4) for i in range(4)]) for shift in (1, 3, 2)
        ]
        stats = merge([stats] + others)
    return stats


def shards(hidden, base_logits, doc_ids, offsets, block_weight, block_bias, projection):
    heads = block_weight.shape[0]
    window = doc_ids.shape[0]
    depth = block_weight.shape[1]
    cols = block_weight.shape[2]
    rows, width = hidden.shape
    core = lax.axis_index("core")
    core_own = core.reshape(1).astype(jnp.int32)
    stretch_index = lax.axis_index(AXES)
    place = jnp.stack([stretch_index * cols // width, stretch_index % (width // cols)]).astype(jnp.int32)

    own_hidden = gather_chips(hidden)
    other_hidden = swap_core(own_hidden).reshape(2, -1, rows, width)
    own_hidden = own_hidden.reshape(2, -1, rows, width)
    base_rows = lax.all_to_all(base_logits, SEQ, split_axis=1, concat_axis=0, tiled=True)

    weight = block_weight.transpose(0, 2, 1).reshape(heads * cols, depth)
    bias = block_bias.reshape(heads * cols, 1)
    proj = projection.T

    position = jnp.arange(window, dtype=jnp.int32)
    shifted = position[None, :] + offsets[:, None]
    padded_ids = jnp.concatenate([doc_ids, jnp.full((4,), -1, jnp.int32)], 0)
    shifted_ids = jnp.stack(
        [lax.dynamic_slice_in_dim(padded_ids, offsets[head], window, 0) for head in range(heads)]
    )
    valid = (shifted_ids == doc_ids[None, :]).reshape(-1)
    order = jnp.arange(heads * window, dtype=jnp.int32)
    rank = jnp.sum(
        jnp.logical_and(valid[:, None], order[:, None] < order[None, :]).astype(jnp.int32), axis=0
    )
    slot = jnp.where(valid, rank, -1)
    count = jnp.sum(valid.astype(jnp.int32))
    by_core = slot.reshape(heads, 2, 2, rows).transpose(0, 2, 1, 3)
    by_core = jnp.where(core == 0, by_core, by_core[:, ::-1])
    slot_here = by_core.reshape(heads, window)

    def branch(size):
        def run(_):
            lanes = jnp.arange(size, dtype=jnp.int32)
            pick = (slot_here[:, :, None] == lanes).astype(BF16)
            source = jnp.sum(
                jnp.where(slot[:, None] == lanes[None, :], shifted.reshape(-1, 1), 0), axis=0
            )
            mask = lanes < count
            pick_base = jnp.logical_and(position[:, None] == source[None, :], mask[None, :])
            target = lax.dot_general(
                base_rows,
                pick_base.astype(F32),
                (((0,), (0,)), ((), ())),
                precision=lax.Precision.HIGHEST,
                preferred_element_type=F32,
            )
            pre, packed = packed_states(place, own_hidden, other_hidden, weight, bias, pick)
            own = gather_chips(packed)
            other = swap_core(own).reshape(-1, size)
            own = own.reshape(-1, size)
            logits, stats = stretch_logits(core_own, proj, own, other, target)
            stats = merge_all(stats)
            top_head, sum_head, top_base, sum_base, cross = [stats[i] for i in range(5)]
            kl = cross / sum_base - (top_base + jnp.log(sum_base)) + (top_head + jnp.log(sum_head))
            loss = jnp.sum(jnp.where(mask, kl, 0.0)) / jnp.maximum(count.astype(F32), 1.0)
            grad = (
                mask.astype(F32)
                * (jnp.exp(logits - top_head) / sum_head - jnp.exp(target - top_base) / sum_base)
            ).astype(BF16)
            theirs = swap_core(state_grad_half(1 - core_own, proj, grad))
            grad_proj = projection_grad(core_own, grad, own, other)
            chip_sum = state_grad_half(core_own, proj, grad, theirs)
            parts = lax.all_to_all(
                chip_sum.reshape(64, cols, size), CHIPS, split_axis=0, concat_axis=0, tiled=True
            )
            state_grad = jnp.sum(parts.reshape(64, cols, size).astype(F32), axis=0)
            grad_block, grad_bias = block_grad(state_grad, pick, pre, own_hidden, other_hidden)
            return grad_proj, grad_block, grad_bias, loss

        return run

    grad_proj, grad_block, grad_bias, loss = lax.cond(
        count <= 384, branch(384), branch(heads * window), 0
    )
    return (
        grad_proj.T,
        grad_block.reshape(heads, cols, depth).transpose(0, 2, 1),
        grad_bias.reshape(heads, cols),
        loss,
    )


def solution(mesh):
    fine = Mesh(mesh.devices.reshape(2, 2, 4, 4, 2), AXES)
    return jax.shard_map(
        shards,
        mesh=fine,
        in_specs=(
            P(SEQ, VOCAB),
            P(SEQ, VOCAB),
            P(),
            P(),
            P(None, None, SEQ + VOCAB),
            P(None, SEQ + VOCAB),
            P(None, VOCAB + SEQ),
        ),
        out_specs=(
            P(None, VOCAB + SEQ),
            P(None, None, SEQ + VOCAB),
            P(None, SEQ + VOCAB),
            P(),
        ),
        check_vma=False,
    )
```

```python
import functools

import jax
import jax.numpy as jnp
from jax import lax
from jax.experimental import pallas as pl
from jax.experimental.pallas import tpu as pltpu
from jax.sharding import Mesh, PartitionSpec as P

AXES = ("zh", "core", "y", "x", "zl")
CHIPS = ("zh", "y", "x", "zl")
SEQ = ("zh", "core")
VOCAB = ("y", "x", "zl")
BF16 = jnp.bfloat16
F32 = jnp.float32
VMEM_LIMIT = 26 * 1024 * 1024
LANES = 128
OWN = {0: 0, 1: 2, 3: 3, 2: 4}
OTHER = {0: 1, 1: 5, 3: 6, 2: 7}
NT = (((1,), (1,)), ((), ()))


def swap_core(x):
    return lax.ppermute(x, "core", [(0, 1), (1, 0)])


def fetch(value, stage, r):
    pairs = []
    for device in range(128):
        zh, core, y, x, zl = device // 64, device // 32 % 2, device // 8 % 4, device // 2 % 4, device % 2
        if stage == 1:
            z = (zh * 2 + zl + r) % 4
            zh, zl = z // 2, z % 2
        elif (stage == 2) == (core == 0):
            x = (x + r) % 4
        else:
            y = (y + r) % 4
        pairs.append((zh * 64 + core * 32 + y * 8 + x * 2 + zl, device))
    return lax.ppermute(value, AXES, pairs)


def params():
    return pltpu.CompilerParams(vmem_limit_bytes=VMEM_LIMIT)


def after(value, *earlier):
    return lax.optimization_barrier((value,) + earlier)[0]


SMEM = pl.BlockSpec(memory_space=pltpu.SMEM)


def whole(array):
    return pl.BlockSpec(array.shape, lambda *_: (0,) * len(array.shape))


def join_kernel(shift_ref, a_ref, b_ref, c_ref, d_ref, out_ref):
    rows = a_ref.shape[0]
    for r, ref in enumerate((a_ref, b_ref, c_ref, d_ref)):
        place = lax.rem(shift_ref[0] + r, 4) * rows
        out_ref[pl.ds(pl.multiple_of(place, rows), rows), :] = ref[...]


def join(shift, parts):
    rows, size = parts[0].shape
    return pl.pallas_call(
        join_kernel,
        in_specs=[SMEM] + [whole(p) for p in parts],
        out_shape=jax.ShapeDtypeStruct((4 * rows, size), parts[0].dtype),
        compiler_params=params(),
        name="join",
    )(shift, *parts)


def sum_cut_kernel(shift_ref, a_ref, b_ref, c_ref, d_ref, *out_refs):
    rows = out_refs[0].shape[0]
    for r, out_ref in enumerate(out_refs):
        place = pl.ds(pl.multiple_of(lax.rem(shift_ref[0] + r, 4) * rows, rows), rows)
        total = a_ref[place, :].astype(F32) + b_ref[place, :].astype(F32)
        total = total + (c_ref[place, :].astype(F32) + d_ref[place, :].astype(F32))
        out_ref[...] = total.astype(BF16)


def sum_cut(shift, parts):
    rows, size = parts[0].shape
    return pl.pallas_call(
        sum_cut_kernel,
        in_specs=[SMEM] + [whole(p) for p in parts],
        out_shape=[jax.ShapeDtypeStruct((rows // 4, size), BF16)] * 4,
        compiler_params=params(),
        name="sum_cut",
    )(shift, *parts)


def gather_pieces(chunk, z_shift, no_shift):
    line = join(z_shift, [chunk] + [fetch(chunk, 1, r) for r in (1, 2, 3)])
    plane = join(no_shift, [line] + [fetch(line, 2, r) for r in (1, 2, 3)])
    return line, plane, {0: plane, **{r: fetch(plane, 3, r) for r in (1, 3, 2)}}


def split_kernel(keep_ref, *refs):
    ins, kept_ref, left_ref = refs[:-2], refs[-2], refs[-1]
    rows, half = ins[0].shape[0], kept_ref.shape[1]
    second = keep_ref[0] == 1
    for index, ref in enumerate(ins):
        a, b = ref[:, :half], ref[:, half:]
        place = slice(index * rows, (index + 1) * rows)
        kept_ref[place, :] = jnp.where(second, b, a)
        left_ref[place, :] = jnp.where(second, a, b)


def split_columns(keep, parts):
    rows, size = parts[0].shape
    return pl.pallas_call(
        split_kernel,
        in_specs=[SMEM] + [whole(p) for p in parts],
        out_shape=[jax.ShapeDtypeStruct((len(parts) * rows, size // 2), F32)] * 2,
        compiler_params=params(),
        name="split_columns",
    )(keep, *parts)


def target_kernel(near_ref, far_ref, pick_ref, out_ref):
    half = near_ref.shape[0]
    total = None
    pieces = []
    for index, ref in enumerate((near_ref, far_ref)):
        pick = pick_ref[index * half : (index + 1) * half, :]
        value = ref[...]
        high = value.astype(BF16)
        rest = value - high.astype(F32)
        middle = rest.astype(BF16)
        low = (rest - middle.astype(F32)).astype(BF16)
        pieces.append((low, middle, high, pick))
    for part in range(3):
        for entry in pieces:
            more = lax.dot_general(
                entry[part], entry[3], (((0,), (0,)), ((), ())), preferred_element_type=F32
            )
            total = more if total is None else total + more
    out_ref[...] = total


def target_rows(near, far, pick):
    return pl.pallas_call(
        target_kernel,
        out_shape=jax.ShapeDtypeStruct((near.shape[1], pick.shape[1]), F32),
        compiler_params=params(),
        name="target_rows",
    )(near, far, pick)


def hidden_block(own_ref, other_ref, i, j, zl, rows):
    def part(ref, at, zh):
        start = (at * 4 + zh * 2 + zl) * rows
        return ref[start : start + rows, :]

    return jnp.concatenate(
        [part(own_ref, j, 0), part(own_ref, j, 1), part(other_ref, i, 0), part(other_ref, i, 1)], axis=0
    )


def states_kernel(place_ref, *refs):
    own_refs, other_refs = refs[:4], refs[4:8]
    weight_ref, bias_ref, pick_ref, pre_ref, packed_ref, near_ref = refs[8:]
    width = own_refs[0].shape[1]
    rows = own_refs[0].shape[0] // 16
    cols = packed_ref.shape[0]
    total = jnp.zeros(pre_ref.shape[::-1], F32)
    for i in range(4):
        for j in range(4):
            where = place_ref[64 + i * 4 + j]
            part = weight_ref[:, pl.ds(pl.multiple_of(where * 2 * width, 2 * width), 2 * width)]
            for zl in range(2):
                block = hidden_block(own_refs[i], other_refs[j], i, j, zl, rows)
                total += lax.dot_general(
                    block, part[:, zl * width : (zl + 1) * width], NT, preferred_element_type=F32
                )

    for i in range(4):
        for j in range(4):

            @pl.when(place_ref[64 + i * 4 + j] == place_ref[80] // 2)
            def _(i=i, j=j):
                for at, (ref, spot) in enumerate([(own_refs[i], j)] * 2 + [(other_refs[j], i)] * 2):
                    start = (spot * 4 + at % 2 * 2 + lax.rem(place_ref[80], 2)) * rows
                    near_ref[at * rows : (at + 1) * rows, :] = ref[pl.ds(pl.multiple_of(start, rows), rows), :]

    lane = lax.broadcasted_iota(jnp.int32, (cols, width), 1)
    row = lax.broadcasted_iota(jnp.int32, (cols, width), 0)
    select = (lane == row + place_ref[81] * cols).astype(BF16)
    own_cols = lax.dot_general(select, near_ref[...], NT, preferred_element_type=F32)

    pre = total.T + bias_ref[...]
    pre_ref[...] = pre
    packed = jnp.zeros(packed_ref.shape, F32)
    for head in range(pick_ref.shape[0]):
        own = pre[head * cols : (head + 1) * cols]
        state = (own_cols + own / (1.0 + jnp.exp(-own))).astype(BF16)
        packed += jnp.dot(state, pick_ref[head], preferred_element_type=F32)
    packed_ref[...] = packed.astype(BF16)


def packed_states(place, own, other, weight, bias, pick):
    heads, window, size = pick.shape
    cols = weight.shape[0] // heads
    args = [own[i] for i in range(4)] + [other[i] for i in range(4)] + [weight, bias, pick]
    return pl.pallas_call(
        states_kernel,
        in_specs=[SMEM] + [whole(a) for a in args],
        out_shape=[
            jax.ShapeDtypeStruct((heads * cols, window), F32),
            jax.ShapeDtypeStruct((cols, size), BF16),
        ],
        scratch_shapes=[pltpu.VMEM((window, own[0].shape[1]), BF16)],
        compiler_params=params(),
        name="packed_states",
    )(place, *args)


def logits_kernel(row, first, last, count, place_ref, proj_ref, *refs):
    pieces, rest = refs[:count], refs[count:]
    total = None
    if not first:
        total, rest = rest[0][...], rest[1:]
    if last:
        target_ref, rest = rest[0], rest[1:]
    for index, piece in enumerate(pieces):
        proj = jnp.concatenate(
            [
                proj_ref[:, pl.ds(pl.multiple_of(place_ref[(row + index) * 8 + k] * LANES, LANES), LANES)]
                for k in range(8)
            ],
            axis=1,
        )
        more = jnp.dot(proj, piece[...], preferred_element_type=F32)
        total = more if total is None else total + more
    rest[0][...] = total
    if last:
        logits = total
        target = target_ref[...]
        top_head = jnp.max(logits, axis=0, keepdims=True)
        top_base = jnp.max(target, axis=0, keepdims=True)
        exp_base = jnp.exp(target - top_base)
        sum_head = jnp.sum(jnp.exp(logits - top_head), axis=0, keepdims=True)
        sum_base = jnp.sum(exp_base, axis=0, keepdims=True)
        cross = jnp.sum(exp_base * (target - logits), axis=0, keepdims=True)
        rest[1][...] = jnp.concatenate(
            [top_head, sum_head, top_base, sum_base, cross, jnp.zeros((3, cross.shape[1]), F32)], 0
        )


def add_logits(place, proj, row, pieces, before=None, target=None):
    stretch = proj.shape[0]
    size = pieces[0].shape[1]
    count = len(pieces)
    args = [proj] + list(pieces) + ([] if before is None else [before]) + ([] if target is None else [target])
    out_shape = [jax.ShapeDtypeStruct((stretch, size), F32)]
    if target is not None:
        out_shape.append(jax.ShapeDtypeStruct((8, size), F32))
    return pl.pallas_call(
        functools.partial(logits_kernel, row, before is None, target is not None, count),
        in_specs=[SMEM] + [whole(a) for a in args],
        out_shape=out_shape,
        compiler_params=params(),
        cost_estimate=pl.CostEstimate(
            flops=count * 2048 * stretch * size,
            bytes_accessed=count * 2048 * (stretch + size),
            transcendentals=0,
        ),
        name="add_logits",
    )(place, *args)


def pair_kernel(a_ref, b_ref, out_ref):
    size = a_ref.shape[1]
    a, b = a_ref[...], b_ref[...]
    top_head = jnp.maximum(a[0:1], b[0:1])
    top_base = jnp.maximum(a[2:3], b[2:3])
    ah, bh = jnp.exp(a[0:1] - top_head), jnp.exp(b[0:1] - top_head)
    ab, bb = jnp.exp(a[2:3] - top_base), jnp.exp(b[2:3] - top_base)
    merged = (
        top_head,
        a[1:2] * ah + b[1:2] * bh,
        top_base,
        a[3:4] * ab + b[3:4] * bb,
        a[4:5] * ab + b[4:5] * bb,
    )
    groups = size // LANES
    rows = [m[:, g * LANES : (g + 1) * LANES] for m in merged for g in range(groups)]
    pad = out_ref.shape[1] - len(rows)
    packed = jnp.concatenate(rows + [jnp.zeros((pad, LANES), F32)], axis=0)
    for index in range(out_ref.shape[0]):
        out_ref[index] = packed


def finish_kernel(count_ref, parts_ref, logits_ref, target_ref, grad_ref, loss_ref):
    size = logits_ref.shape[1]
    groups = size // LANES
    parts = parts_ref[...]

    def rows(k):
        return parts[:, k * groups : (k + 1) * groups, :]

    def flat(value):
        return jnp.concatenate([value[g : g + 1, :] for g in range(groups)], axis=1)

    top_head = jnp.max(rows(0), axis=0)
    top_base = jnp.max(rows(2), axis=0)
    head = jnp.exp(rows(0) - top_head[None])
    base = jnp.exp(rows(2) - top_base[None])
    sum_head = flat(jnp.sum(rows(1) * head, axis=0))
    sum_base = flat(jnp.sum(rows(3) * base, axis=0))
    cross = flat(jnp.sum(rows(4) * base, axis=0))
    top_head, top_base = flat(top_head), flat(top_base)
    mask = lax.broadcasted_iota(jnp.int32, (1, size), 1) < count_ref[0]
    kl = cross / sum_base - (top_base + jnp.log(sum_base)) + (top_head + jnp.log(sum_head))
    total = jnp.sum(jnp.where(mask, kl, 0.0), axis=1, keepdims=True)
    loss_ref[...] = total / jnp.maximum(count_ref[0].astype(F32), 1.0)
    keep = mask.astype(F32)
    grad_ref[...] = (
        keep
        * (
            jnp.exp(logits_ref[...] - top_head) * (1.0 / sum_head)
            - jnp.exp(target_ref[...] - top_base) * (1.0 / sum_base)
        )
    ).astype(BF16)


def logits_grad(stats, logits, target, count):
    size = stats.shape[1]
    rows = -(-5 * (size // LANES) // 8) * 8
    packed = pl.pallas_call(
        pair_kernel,
        out_shape=jax.ShapeDtypeStruct((64, rows, LANES), F32),
        compiler_params=params(),
        name="merge_pair",
    )(stats, swap_core(stats))
    parts = lax.all_to_all(packed, CHIPS, split_axis=0, concat_axis=0, tiled=True)
    args = [parts, logits, target]
    return pl.pallas_call(
        finish_kernel,
        in_specs=[SMEM] + [whole(a) for a in args],
        out_shape=[
            jax.ShapeDtypeStruct(logits.shape, BF16),
            jax.ShapeDtypeStruct((1, 1), F32),
        ],
        compiler_params=params(),
        name="logits_grad",
    )(count.reshape(1), *args)


def turn_kernel(proj_ref, out_ref):
    @pl.loop(0, proj_ref.shape[1] // 512)
    def _(index):
        place = pl.ds(pl.multiple_of(index * 512, 512), 512)
        out_ref[place, :] = proj_ref[:, place].T


def turned(proj):
    stretch, depth = proj.shape
    return pl.pallas_call(
        turn_kernel,
        in_specs=[whole(proj)],
        out_shape=jax.ShapeDtypeStruct((depth, stretch), proj.dtype),
        compiler_params=params(),
        cost_estimate=pl.CostEstimate(flops=0, bytes_accessed=4 * depth * stretch, transcendentals=0),
        name="turned",
    )(proj)


def state_grad_kernel(row, place_ref, proj_ref, grad_ref, *refs):
    blocks = [
        proj_ref[pl.ds(pl.multiple_of(place_ref[row * 8 + k] * LANES, LANES), LANES), :] for k in range(8)
    ]
    total = jnp.dot(jnp.concatenate(blocks, axis=0), grad_ref[...], preferred_element_type=F32)
    if len(refs) == 2:
        total = total + refs[0][...].astype(F32)
    refs[-1][...] = total.astype(BF16)


def state_grad_piece(place, proj, row, grad, *add):
    stretch = proj.shape[1]
    size = grad.shape[1]
    args = [proj, grad] + list(add)
    return pl.pallas_call(
        functools.partial(state_grad_kernel, row),
        in_specs=[SMEM] + [whole(a) for a in args],
        out_shape=jax.ShapeDtypeStruct((8 * LANES, size), BF16),
        compiler_params=params(),
        cost_estimate=pl.CostEstimate(
            flops=2048 * stretch * size, bytes_accessed=2048 * (stretch + size), transcendentals=0
        ),
        name="state_grad_piece",
    )(place, *args)


def grad_proj_kernel(place_ref, grad_ref, *refs):
    pieces, out_ref, slots_ref, sem = refs[:8], refs[8], refs[9], refs[10]

    def copy(row, k):
        place = pl.multiple_of(place_ref[row * 8 + k] * LANES, LANES)
        return pltpu.make_async_copy(
            slots_ref.at[row % 2, :, pl.ds(k * LANES, LANES)],
            out_ref.at[:, pl.ds(place, LANES)],
            sem.at[row % 2, k],
        )

    for row, piece in enumerate(pieces):
        if row >= 2:
            for k in range(8):
                copy(row - 2, k).wait()
        slots_ref[row % 2] = lax.dot_general(
            grad_ref[...], piece[...], NT, preferred_element_type=F32
        ).astype(BF16)
        for k in range(8):
            copy(row, k).start()
    for row in (len(pieces) - 2, len(pieces) - 1):
        for k in range(8):
            copy(row, k).wait()


def projection_grad(place, grad, pieces):
    stretch, size = grad.shape
    rows = pieces[0].shape[0]
    depth = 8 * rows
    return pl.pallas_call(
        grad_proj_kernel,
        in_specs=[SMEM, whole(grad)] + [whole(p) for p in pieces],
        out_specs=pl.BlockSpec(memory_space=pl.ANY),
        out_shape=jax.ShapeDtypeStruct((stretch, depth), BF16),
        scratch_shapes=[pltpu.VMEM((2, stretch, rows), BF16), pltpu.SemaphoreType.DMA((2, 8))],
        compiler_params=params(),
        cost_estimate=pl.CostEstimate(
            flops=2 * stretch * depth * size, bytes_accessed=2 * depth * (stretch + size), transcendentals=0
        ),
        name="projection_grad",
    )(place, grad, *pieces)


def grad_block_kernel(place_ref, *refs):
    sums, pick_ref, pre_ref, own_refs, other_refs = refs[:4], refs[4], refs[5], refs[6:10], refs[10:14]
    out_ref, bias_ref, pre_grad_ref = refs[14:]
    width = own_refs[0].shape[1]
    rows = own_refs[0].shape[0] // 16
    cols = sums[0].shape[0]
    total = sums[0][...].astype(F32) + sums[1][...].astype(F32)
    total = total + (sums[2][...].astype(F32) + sums[3][...].astype(F32))
    high = total.astype(BF16)
    rest = total - high.astype(F32)
    middle = rest.astype(BF16)
    low = (rest - middle.astype(F32)).astype(BF16)
    for head in range(pick_ref.shape[0]):
        own = slice(head * cols, (head + 1) * cols)
        spread = sum(
            lax.dot_general(piece, pick_ref[head], NT, preferred_element_type=F32)
            for piece in (low, middle, high)
        )
        pre = pre_ref[own]
        sigma = 1.0 / (1.0 + jnp.exp(-pre))
        pre_grad = spread * (sigma * (1.0 + pre * (1.0 - sigma)))
        bias_ref[head : head + 1, :] = jnp.sum(pre_grad.T, axis=0, keepdims=True)
        pre_grad_ref[own] = pre_grad.astype(BF16)
    grad = pre_grad_ref[...]
    for i in range(4):
        for j in range(4):
            halves = [
                jnp.dot(
                    grad,
                    hidden_block(own_refs[i], other_refs[j], i, j, zl, rows),
                    preferred_element_type=F32,
                ).astype(BF16)
                for zl in range(2)
            ]
            place = pl.multiple_of(place_ref[64 + i * 4 + j] * 2 * width, 2 * width)
            out_ref[:, pl.ds(place, 2 * width)] = jnp.concatenate(halves, axis=1)


def block_grad(place, sums, pick, pre, own, other, depth):
    heads, window, size = pick.shape
    cols = sums[0].shape[0]
    args = list(sums) + [pick, pre] + [own[i] for i in range(4)] + [other[i] for i in range(4)]
    return pl.pallas_call(
        grad_block_kernel,
        in_specs=[SMEM] + [whole(a) for a in args],
        out_shape=[
            jax.ShapeDtypeStruct((heads * cols, depth), BF16),
            jax.ShapeDtypeStruct((heads, cols), F32),
        ],
        scratch_shapes=[pltpu.VMEM((heads * cols, window), BF16)],
        compiler_params=params(),
        name="block_grad",
    )(place, *args)


def places(core, y, x, stretch_index, share):
    def chain(which):
        third = jnp.arange(4)[:, None, None]
        second = jnp.arange(4)[None, :, None]
        zh = jnp.arange(2)[None, None, :]
        y_at = (y + jnp.where(which == 0, third, second)) % 4
        x_at = (x + jnp.where(which == 0, second, third)) % 4
        plane = y_at * 4 + x_at
        return (zh * 32 + which * 16 + plane).reshape(4, 8), plane.reshape(16)

    own, plane = chain(core)
    other, _ = chain(1 - core)
    rows = [own[0], other[0], own[1], own[3], own[2], other[1], other[3], other[2]]
    tail = jnp.stack([stretch_index // share, stretch_index % share])
    return jnp.concatenate(rows + [plane, tail]).astype(jnp.int32)


def shards(hidden, base_logits, doc_ids, offsets, block_weight, block_bias, projection):
    heads, depth, cols = block_weight.shape
    window = doc_ids.shape[0]
    rows, width = hidden.shape
    zh, core, y, x, zl = [lax.axis_index(a) for a in AXES]
    stretch_index = lax.axis_index(AXES)
    place = places(core, y, x, stretch_index, width // cols)
    z_shift = (zh * 2 + zl).reshape(1).astype(jnp.int32)
    no_shift = jnp.zeros((1,), jnp.int32)

    weight = block_weight.transpose(0, 2, 1).reshape(heads * cols, depth)
    bias = block_bias.reshape(heads * cols, 1)
    proj = projection.T

    position = jnp.arange(window, dtype=jnp.int32)
    local = jnp.arange(rows, dtype=jnp.int32)
    base_position = jnp.concatenate(
        [((zh ^ a) * 2 + (core ^ b)) * rows + local for b in range(2) for a in range(2)]
    )
    shifted = position[None, :] + offsets[:, None]
    padded_ids = jnp.concatenate([doc_ids, jnp.full((4,), -1, jnp.int32)], 0)
    shifted_ids = jnp.stack(
        [lax.dynamic_slice_in_dim(padded_ids, offsets[head], window, 0) for head in range(heads)]
    )
    valid = (shifted_ids == doc_ids[None, :]).reshape(-1)
    order = jnp.arange(heads * window, dtype=jnp.int32)
    rank = jnp.sum(
        jnp.logical_and(valid[:, None], order[:, None] < order[None, :]).astype(jnp.int32), axis=0
    )
    slot = jnp.where(valid, rank, -1)
    count = jnp.sum(valid.astype(jnp.int32))
    by_core = slot.reshape(heads, 2, 2, rows).transpose(0, 2, 1, 3)
    by_core = jnp.where(core == 0, by_core, by_core[:, ::-1])
    slot_here = by_core.reshape(heads, window)

    def branch(size):
        def run(hidden, base_logits, proj, weight):
            line, plane, own_hidden = gather_pieces(hidden, z_shift, no_shift)
            other_hidden = {r: swap_core(own_hidden[r]) for r in (0, 1, 3, 2)}
            lanes = jnp.arange(size, dtype=jnp.int32)
            pick = (slot_here[:, :, None] == lanes).astype(BF16)
            source = jnp.sum(
                jnp.where(slot[:, None] == lanes[None, :], shifted.reshape(-1, 1), 0), axis=0
            )
            mask = lanes < count
            pick_base = jnp.logical_and(base_position[:, None] == source[None, :], mask[None, :]).astype(BF16)
            pre, packed = packed_states(place, own_hidden, other_hidden, weight, bias, pick)
            line, plane, own = gather_pieces(packed, z_shift, no_shift)
            other = {0: swap_core(plane)}
            kept, left = split_columns(zh.reshape(1), [after(base_logits, line)])
            came = lax.ppermute(left, "zh", [(0, 1), (1, 0)])
            kept, left = split_columns(core.reshape(1), [kept, came])
            target = target_rows(kept, swap_core(left), pick_base)
            logits = add_logits(place, proj, 0, [own[0], other[0]])[0]
            proj_turned = turned(after(proj, plane))
            for r in (1, 3, 2):
                own[r] = after(own[r], logits, proj_turned)
                other[r] = swap_core(own[r])
            logits = add_logits(place, proj, 2, [own[r] for r in (1, 3, 2)], logits)[0]
            logits, stats = add_logits(place, proj, 5, [other[r] for r in (1, 3, 2)], logits, target)
            grad, loss = logits_grad(stats, logits, target, count)

            sent = {
                r: swap_core(state_grad_piece(place, proj_turned, OTHER[r], grad)) for r in (1, 3, 2, 0)
            }
            parts = []
            for r in (1, 3, 2, 0):
                piece = state_grad_piece(place, proj_turned, OWN[r], grad, sent[r])
                parts.append(piece if r == 0 else fetch(piece, 3, 4 - r))
            pieces = [own[0], other[0]] + [own[r] for r in (1, 3, 2)] + [other[r] for r in (1, 3, 2)]
            grad_proj = projection_grad(place, after(grad, piece), pieces)
            parts = [after(p, grad_proj) for p in parts]
            parts = sum_cut(no_shift, parts)
            parts = sum_cut(z_shift, [parts[0]] + [fetch(parts[r], 2, 4 - r) for r in (1, 3, 2)])
            sums = [parts[0]] + [fetch(parts[r], 1, 4 - r) for r in (1, 3, 2)]

            grad_block, grad_bias = block_grad(place, sums, pick, pre, own_hidden, other_hidden, depth)
            return grad_proj, grad_block, grad_bias, loss.reshape(())

        return run

    args = (hidden, base_logits, proj, weight)
    packed_size = 384
    result = branch(packed_size)(*args)
    grad_proj, grad_block, grad_bias, loss = lax.cond(
        count <= packed_size, lambda done, args: done, lambda done, args: branch(heads * window)(*args), result, args
    )
    return (
        grad_proj.T,
        grad_block.reshape(heads, cols, depth).transpose(0, 2, 1),
        grad_bias,
        loss,
    )


def solution(mesh):
    fine = Mesh(mesh.devices.reshape(2, 2, 4, 4, 2), AXES)
    return jax.shard_map(
        shards,
        mesh=fine,
        in_specs=(
            P(SEQ, VOCAB),
            P(SEQ, VOCAB),
            P(),
            P(),
            P(None, None, SEQ + VOCAB),
            P(None, SEQ + VOCAB),
            P(None, VOCAB + SEQ),
        ),
        out_specs=(
            P(None, VOCAB + SEQ),
            P(None, None, SEQ + VOCAB),
            P(None, SEQ + VOCAB),
            P(),
        ),
        check_vma=False,
    )
```

```python
import functools

import jax
import jax.numpy as jnp
from jax import lax
from jax.experimental import pallas as pl
from jax.experimental.pallas import tpu as pltpu
from jax.sharding import Mesh, PartitionSpec as P

AXES = ("zh", "core", "y", "x", "zl")
CHIPS = ("zh", "y", "x", "zl")
SEQ = ("zh", "core")
VOCAB = ("y", "x", "zl")
BF16 = jnp.bfloat16
F32 = jnp.float32
VMEM_LIMIT = 18 * 1024 * 1024
LANES = 128
OWN = {0: 0, 1: 2, 3: 3, 2: 4}
OTHER = {0: 1, 1: 5, 3: 6, 2: 7}
NT = (((1,), (1,)), ((), ()))


def swap_core(x):
    return lax.ppermute(x, "core", [(0, 1), (1, 0)])


def fetch(value, stage, r):
    pairs = []
    for device in range(128):
        zh, core, y, x, zl = device // 64, device // 32 % 2, device // 8 % 4, device // 2 % 4, device % 2
        if stage == 1:
            z = (zh * 2 + zl + r) % 4
            zh, zl = z // 2, z % 2
        elif (stage == 2) == (core == 0):
            x = (x + r) % 4
        else:
            y = (y + r) % 4
        pairs.append((zh * 64 + core * 32 + y * 8 + x * 2 + zl, device))
    return lax.ppermute(value, AXES, pairs)


def params(limit=VMEM_LIMIT):
    return pltpu.CompilerParams(vmem_limit_bytes=limit)


def after(value, *earlier):
    return lax.optimization_barrier((value,) + earlier)[0]


SMEM = pl.BlockSpec(memory_space=pltpu.SMEM)
SMALL = pl.CostEstimate(flops=1, bytes_accessed=1, transcendentals=0)


def whole(array):
    return pl.BlockSpec(array.shape, lambda *_: (0,) * len(array.shape))


def join_kernel(shift_ref, a_ref, b_ref, c_ref, d_ref, out_ref):
    rows = a_ref.shape[0]
    for r, ref in enumerate((a_ref, b_ref, c_ref, d_ref)):
        place = lax.rem(shift_ref[0] + r, 4) * rows
        out_ref[pl.ds(pl.multiple_of(place, rows), rows), :] = ref[...]


def join(shift, parts):
    rows, size = parts[0].shape
    return pl.pallas_call(
        join_kernel,
        in_specs=[SMEM] + [whole(p) for p in parts],
        out_shape=jax.ShapeDtypeStruct((4 * rows, size), parts[0].dtype),
        compiler_params=params(),
        name="join",
    )(shift, *parts)


def sum_cut_kernel(shift_ref, a_ref, b_ref, c_ref, d_ref, *out_refs):
    rows = out_refs[0].shape[0]
    for r, out_ref in enumerate(out_refs):
        place = pl.ds(pl.multiple_of(lax.rem(shift_ref[0] + r, 4) * rows, rows), rows)
        total = a_ref[place, :].astype(F32) + b_ref[place, :].astype(F32)
        total = total + (c_ref[place, :].astype(F32) + d_ref[place, :].astype(F32))
        out_ref[...] = total.astype(BF16)


def sum_cut(shift, parts):
    rows, size = parts[0].shape
    return pl.pallas_call(
        sum_cut_kernel,
        in_specs=[SMEM] + [whole(p) for p in parts],
        out_shape=[jax.ShapeDtypeStruct((rows // 4, size), BF16)] * 4,
        compiler_params=params(),
        name="sum_cut",
    )(shift, *parts)


def gather_plane(chunk, z_shift, no_shift):
    line = join(z_shift, [chunk] + [fetch(chunk, 1, r) for r in (1, 2, 3)])
    return join(no_shift, [line] + [fetch(line, 2, r) for r in (1, 2, 3)])


def split_kernel(keep_ref, *refs):
    ins, kept_ref, left_ref = refs[:-2], refs[-2], refs[-1]
    rows, half = ins[0].shape[0], kept_ref.shape[1]
    second = keep_ref[0] == 1
    for index, ref in enumerate(ins):
        a, b = ref[:, :half], ref[:, half:]
        place = slice(index * rows, (index + 1) * rows)
        kept_ref[place, :] = jnp.where(second, b, a)
        left_ref[place, :] = jnp.where(second, a, b)


def split_columns(keep, parts):
    rows, size = parts[0].shape
    return pl.pallas_call(
        split_kernel,
        in_specs=[SMEM] + [whole(p) for p in parts],
        out_shape=[jax.ShapeDtypeStruct((len(parts) * rows, size // 2), F32)] * 2,
        compiler_params=params(),
        name="split_columns",
    )(keep, *parts)


def target_kernel(near_ref, far_ref, pick_ref, out_ref):
    half = near_ref.shape[0]
    total = None
    pieces = []
    for index, ref in enumerate((near_ref, far_ref)):
        pick = pick_ref[index * half : (index + 1) * half, :]
        value = ref[...]
        high = value.astype(BF16)
        rest = value - high.astype(F32)
        middle = rest.astype(BF16)
        low = (rest - middle.astype(F32)).astype(BF16)
        pieces.append((low, middle, high, pick))
    for part in range(3):
        for entry in pieces:
            more = lax.dot_general(
                entry[part], entry[3], (((0,), (0,)), ((), ())), preferred_element_type=F32
            )
            total = more if total is None else total + more
    out_ref[...] = total


def target_rows(near, far, pick):
    return pl.pallas_call(
        target_kernel,
        out_shape=jax.ShapeDtypeStruct((near.shape[1], pick.shape[1]), F32),
        compiler_params=params(),
        name="target_rows",
    )(near, far, pick)


def hidden_block(own_ref, other_ref, i, j, zl, rows):
    def part(ref, at, zh):
        start = (at * 4 + zh * 2 + zl) * rows
        return ref[start : start + rows, :]

    return jnp.concatenate(
        [part(own_ref, j, 0), part(own_ref, j, 1), part(other_ref, i, 0), part(other_ref, i, 1)], axis=0
    )


def states_kernel(place_ref, *refs):
    own_refs, other_refs = refs[:4], refs[4:8]
    weight_ref, bias_ref, pick_ref, pre_ref, packed_ref, near_ref = refs[8:]
    width = own_refs[0].shape[1]
    rows = own_refs[0].shape[0] // 16
    cols = packed_ref.shape[0]
    total = jnp.zeros(pre_ref.shape[::-1], F32)
    for i in range(4):
        for j in range(4):
            where = place_ref[64 + i * 4 + j]
            part = weight_ref[:, pl.ds(pl.multiple_of(where * 2 * width, 2 * width), 2 * width)]
            for zl in range(2):
                block = hidden_block(own_refs[i], other_refs[j], i, j, zl, rows)
                total += lax.dot_general(
                    block, part[:, zl * width : (zl + 1) * width], NT, preferred_element_type=F32
                )

    for i in range(4):
        for j in range(4):

            @pl.when(place_ref[64 + i * 4 + j] == place_ref[80] // 2)
            def _(i=i, j=j):
                for at, (ref, spot) in enumerate([(own_refs[i], j)] * 2 + [(other_refs[j], i)] * 2):
                    start = (spot * 4 + at % 2 * 2 + lax.rem(place_ref[80], 2)) * rows
                    near_ref[at * rows : (at + 1) * rows, :] = ref[pl.ds(pl.multiple_of(start, rows), rows), :]

    lane = lax.broadcasted_iota(jnp.int32, (cols, width), 1)
    row = lax.broadcasted_iota(jnp.int32, (cols, width), 0)
    select = (lane == row + place_ref[81] * cols).astype(BF16)
    own_cols = lax.dot_general(select, near_ref[...], NT, preferred_element_type=F32)

    bias = jnp.concatenate([bias_ref[head : head + 1, :] for head in range(pick_ref.shape[0])], axis=1)
    pre = (total + bias).T
    pre_ref[...] = pre
    packed = jnp.zeros(packed_ref.shape, F32)
    for head in range(pick_ref.shape[0]):
        own = pre[head * cols : (head + 1) * cols]
        state = (own_cols + own / (1.0 + jnp.exp(-own))).astype(BF16)
        packed += jnp.dot(state, pick_ref[head], preferred_element_type=F32)
    packed_ref[...] = packed.astype(BF16)


def packed_states(place, own, other, weight, bias, pick):
    heads, window, size = pick.shape
    cols = weight.shape[0] // heads
    args = [own[i] for i in range(4)] + [other[i] for i in range(4)] + [weight, bias, pick]
    return pl.pallas_call(
        states_kernel,
        in_specs=[SMEM] + [whole(a) for a in args],
        out_shape=[
            jax.ShapeDtypeStruct((heads * cols, window), F32),
            jax.ShapeDtypeStruct((cols, size), BF16),
        ],
        scratch_shapes=[pltpu.VMEM((window, own[0].shape[1]), BF16)],
        compiler_params=params(),
        name="packed_states",
    )(place, *args)


def logits_kernel(row, first, last, count, place_ref, proj_ref, *refs):
    pieces, rest = refs[:count], refs[count:]
    total = None
    if not first:
        total, rest = rest[0][...], rest[1:]
    if last:
        target_ref, rest = rest[0], rest[1:]
    for index, piece in enumerate(pieces):
        proj = jnp.concatenate(
            [
                proj_ref[:, pl.ds(pl.multiple_of(place_ref[(row + index) * 8 + k] * LANES, LANES), LANES)]
                for k in range(8)
            ],
            axis=1,
        )
        more = jnp.dot(proj, piece[...], preferred_element_type=F32)
        total = more if total is None else total + more
    rest[0][...] = total
    if last:
        logits = total
        target = target_ref[...]
        top_head = jnp.max(logits, axis=0, keepdims=True)
        top_base = jnp.max(target, axis=0, keepdims=True)
        exp_base = jnp.exp(target - top_base)
        sum_head = jnp.sum(jnp.exp(logits - top_head), axis=0, keepdims=True)
        sum_base = jnp.sum(exp_base, axis=0, keepdims=True)
        cross = jnp.sum(exp_base * (target - logits), axis=0, keepdims=True)
        rest[1][...] = jnp.concatenate(
            [top_head, sum_head, top_base, sum_base, cross, jnp.zeros((3, cross.shape[1]), F32)], 0
        )


def add_logits(place, proj, row, pieces, before=None, target=None):
    stretch = proj.shape[0]
    size = pieces[0].shape[1]
    count = len(pieces)
    args = [proj] + list(pieces) + ([] if before is None else [before]) + ([] if target is None else [target])
    out_shape = [jax.ShapeDtypeStruct((stretch, size), F32)]
    if target is not None:
        out_shape.append(jax.ShapeDtypeStruct((8, size), F32))
    return pl.pallas_call(
        functools.partial(logits_kernel, row, before is None, target is not None, count),
        in_specs=[SMEM] + [whole(a) for a in args],
        out_shape=out_shape,
        compiler_params=params(),
        cost_estimate=SMALL,
        name="add_logits",
    )(place, *args)


def pair_kernel(a_ref, b_ref, out_ref):
    size = a_ref.shape[1]
    a, b = a_ref[...], b_ref[...]
    top_head = jnp.maximum(a[0:1], b[0:1])
    top_base = jnp.maximum(a[2:3], b[2:3])
    ah, bh = jnp.exp(a[0:1] - top_head), jnp.exp(b[0:1] - top_head)
    ab, bb = jnp.exp(a[2:3] - top_base), jnp.exp(b[2:3] - top_base)
    merged = (
        top_head,
        a[1:2] * ah + b[1:2] * bh,
        top_base,
        a[3:4] * ab + b[3:4] * bb,
        a[4:5] * ab + b[4:5] * bb,
    )
    groups = size // LANES
    rows = [m[:, g * LANES : (g + 1) * LANES] for m in merged for g in range(groups)]
    pad = out_ref.shape[1] - len(rows)
    packed = jnp.concatenate(rows + [jnp.zeros((pad, LANES), F32)], axis=0)
    for index in range(out_ref.shape[0]):
        out_ref[index] = packed


def finish_kernel(count_ref, parts_ref, logits_ref, target_ref, grad_ref, loss_ref):
    size = logits_ref.shape[1]
    groups = size // LANES
    parts = parts_ref[...]

    def rows(k):
        return parts[:, k * groups : (k + 1) * groups, :]

    def flat(value):
        return jnp.concatenate([value[g : g + 1, :] for g in range(groups)], axis=1)

    top_head = jnp.max(rows(0), axis=0)
    top_base = jnp.max(rows(2), axis=0)
    head = jnp.exp(rows(0) - top_head[None])
    base = jnp.exp(rows(2) - top_base[None])
    sum_head = flat(jnp.sum(rows(1) * head, axis=0))
    sum_base = flat(jnp.sum(rows(3) * base, axis=0))
    cross = flat(jnp.sum(rows(4) * base, axis=0))
    top_head, top_base = flat(top_head), flat(top_base)
    mask = lax.broadcasted_iota(jnp.int32, (1, size), 1) < count_ref[0]
    kl = cross / sum_base - (top_base + jnp.log(sum_base)) + (top_head + jnp.log(sum_head))
    total = jnp.sum(jnp.where(mask, kl, 0.0), axis=1, keepdims=True)
    loss_ref[...] = total / jnp.maximum(count_ref[0].astype(F32), 1.0)
    keep = mask.astype(F32)
    grad_ref[...] = (
        keep
        * (
            jnp.exp(logits_ref[...] - top_head) * (1.0 / sum_head)
            - jnp.exp(target_ref[...] - top_base) * (1.0 / sum_base)
        )
    ).astype(BF16)


def logits_grad(stats, logits, target, count):
    size = stats.shape[1]
    rows = -(-5 * (size // LANES) // 8) * 8
    packed = pl.pallas_call(
        pair_kernel,
        out_shape=jax.ShapeDtypeStruct((64, rows, LANES), F32),
        compiler_params=params(),
        name="merge_pair",
    )(stats, swap_core(stats))
    parts = lax.all_to_all(packed, CHIPS, split_axis=0, concat_axis=0, tiled=True)
    args = [parts, logits, target]
    return pl.pallas_call(
        finish_kernel,
        in_specs=[SMEM] + [whole(a) for a in args],
        out_shape=[
            jax.ShapeDtypeStruct(logits.shape, BF16),
            jax.ShapeDtypeStruct((1, 1), F32),
        ],
        compiler_params=params(),
        name="logits_grad",
    )(count, *args)


def turn_kernel(proj_ref, out_ref):
    @pl.loop(0, proj_ref.shape[1] // 512)
    def _(index):
        place = pl.ds(pl.multiple_of(index * 512, 512), 512)
        out_ref[place, :] = proj_ref[:, place].T


def turned(proj):
    stretch, depth = proj.shape
    return pl.pallas_call(
        turn_kernel,
        in_specs=[whole(proj)],
        out_shape=jax.ShapeDtypeStruct((depth, stretch), proj.dtype),
        compiler_params=params(26 * 1024 * 1024),
        cost_estimate=SMALL,
        name="turned",
    )(proj)


def state_grad_kernel(row, place_ref, proj_ref, grad_ref, *refs):
    blocks = [
        proj_ref[pl.ds(pl.multiple_of(place_ref[row * 8 + k] * LANES, LANES), LANES), :] for k in range(8)
    ]
    total = jnp.dot(jnp.concatenate(blocks, axis=0), grad_ref[...], preferred_element_type=F32)
    if len(refs) == 2:
        total = total + refs[0][...].astype(F32)
    refs[-1][...] = total.astype(BF16)


def state_grad_piece(place, proj, row, grad, *add):
    stretch = proj.shape[1]
    size = grad.shape[1]
    args = [proj, grad] + list(add)
    return pl.pallas_call(
        functools.partial(state_grad_kernel, row),
        in_specs=[SMEM] + [whole(a) for a in args],
        out_shape=jax.ShapeDtypeStruct((8 * LANES, size), BF16),
        compiler_params=params(),
        cost_estimate=SMALL,
        name="state_grad_piece",
    )(place, *args)


def grad_proj_kernel(rows, place_ref, grad_ref, *refs):
    pieces, (out_ref, slots_ref, sem) = refs[: len(rows)], refs[-3:]

    def copy(step, k):
        place = pl.multiple_of(place_ref[rows[step] * 8 + k] * LANES, LANES)
        return pltpu.make_async_copy(
            slots_ref.at[step % 2, :, pl.ds(k * LANES, LANES)],
            out_ref.at[:, pl.ds(place, LANES)],
            sem.at[step % 2, k],
        )

    for step, piece in enumerate(pieces):
        if step >= 2:
            for k in range(8):
                copy(step - 2, k).wait()
        slots_ref[step % 2] = lax.dot_general(
            grad_ref[...], piece[...], NT, preferred_element_type=F32
        ).astype(BF16)
        for k in range(8):
            copy(step, k).start()
    for step in range(max(len(rows) - 2, 0), len(rows)):
        for k in range(8):
            copy(step, k).wait()


def projection_grad(place, grad, depth, rows, pieces, before=None):
    stretch, size = grad.shape
    height = pieces[0].shape[0]
    anywhere = pl.BlockSpec(memory_space=pltpu.HBM)
    more = [] if before is None else [before]
    return pl.pallas_call(
        functools.partial(grad_proj_kernel, rows),
        in_specs=[SMEM, whole(grad)] + [whole(p) for p in pieces] + [anywhere] * len(more),
        out_specs=anywhere,
        out_shape=jax.ShapeDtypeStruct((stretch, depth), BF16),
        scratch_shapes=[pltpu.VMEM((2, stretch, height), BF16), pltpu.SemaphoreType.DMA((2, 8))],
        input_output_aliases={} if before is None else {2 + len(pieces): 0},
        compiler_params=params(),
        cost_estimate=SMALL,
        name="projection_grad",
    )(place, grad, *pieces, *more)


def grad_block_kernel(place_ref, *refs):
    sums, pick_ref, pre_ref, own_refs, other_refs = refs[:4], refs[4], refs[5], refs[6:10], refs[10:14]
    out_ref, bias_ref, pre_grad_ref = refs[14:]
    width = own_refs[0].shape[1]
    rows = own_refs[0].shape[0] // 16
    cols = sums[0].shape[0]
    total = sums[0][...].astype(F32) + sums[1][...].astype(F32)
    total = total + (sums[2][...].astype(F32) + sums[3][...].astype(F32))
    high = total.astype(BF16)
    rest = total - high.astype(F32)
    middle = rest.astype(BF16)
    low = (rest - middle.astype(F32)).astype(BF16)
    for head in range(pick_ref.shape[0]):
        own = slice(head * cols, (head + 1) * cols)
        spread = sum(
            lax.dot_general(piece, pick_ref[head], NT, preferred_element_type=F32)
            for piece in (low, middle, high)
        )
        pre = pre_ref[own]
        sigma = 1.0 / (1.0 + jnp.exp(-pre))
        pre_grad = spread * (sigma * (1.0 + pre * (1.0 - sigma)))
        bias_ref[head : head + 1, :] = jnp.sum(pre_grad.T, axis=0, keepdims=True)
        pre_grad_ref[own] = pre_grad.astype(BF16)
    grad = pre_grad_ref[...]
    for i in range(4):
        for j in range(4):
            halves = [
                jnp.dot(
                    grad,
                    hidden_block(own_refs[i], other_refs[j], i, j, zl, rows),
                    preferred_element_type=F32,
                ).astype(BF16)
                for zl in range(2)
            ]
            place = pl.multiple_of(place_ref[64 + i * 4 + j] * 2 * width, 2 * width)
            out_ref[:, pl.ds(place, 2 * width)] = jnp.concatenate(halves, axis=1)


def block_grad(place, sums, pick, pre, own, other, depth):
    heads, window, size = pick.shape
    cols = sums[0].shape[0]
    args = list(sums) + [pick, pre] + [own[i] for i in range(4)] + [other[i] for i in range(4)]
    return pl.pallas_call(
        grad_block_kernel,
        in_specs=[SMEM] + [whole(a) for a in args],
        out_shape=[
            jax.ShapeDtypeStruct((heads * cols, depth), BF16),
            jax.ShapeDtypeStruct((heads, cols), F32),
        ],
        scratch_shapes=[pltpu.VMEM((heads * cols, window), BF16)],
        compiler_params=params(),
        name="block_grad",
    )(place, *args)


def place_kernel(share, info_ref, out_ref):
    core, y, x, stretch = [info_ref[k] for k in range(4)]
    for table, which in ((OWN, core), (OTHER, 1 - core)):
        for third in range(4):
            for second in range(4):
                y_at = lax.rem(y + jnp.where(which == 0, third, second), 4)
                x_at = lax.rem(x + jnp.where(which == 0, second, third), 4)
                plane = y_at * 4 + x_at
                for zh in range(2):
                    out_ref[table[third] * 8 + second * 2 + zh] = zh * 32 + which * 16 + plane
                if table is OWN:
                    out_ref[64 + third * 4 + second] = plane
    out_ref[80] = stretch // share
    out_ref[81] = lax.rem(stretch, share)


def places(core, y, x, stretch_index, share):
    return pl.pallas_call(
        functools.partial(place_kernel, share),
        in_specs=[SMEM],
        out_specs=SMEM,
        out_shape=jax.ShapeDtypeStruct((82,), jnp.int32),
        name="places",
    )(jnp.stack([core, y, x, stretch_index]).astype(jnp.int32))


def rows_kernel(info_ref, offsets_ref, ids_ref, pick_ref, base_ref, count_ref):
    heads, window, size = pick_ref.shape
    core, zh = info_ref[0], info_ref[1]
    block = window // 4
    ids = ids_ref[...]
    valid = []
    for head in range(heads):
        later = jnp.full(ids.shape, -1, jnp.int32)
        for k in range(1, 5):
            moved = jnp.concatenate([ids[:, k:], jnp.full((1, k), -1, jnp.int32)], axis=1)
            later = jnp.where(offsets_ref[head] == k, moved, later)
        valid.append(jnp.where(later == ids, 1.0, 0.0))
    flat = jnp.concatenate(valid, axis=1)
    count_ref[0] = jnp.sum(flat).astype(jnp.int32)
    length = heads * window
    before = lax.broadcasted_iota(jnp.int32, (length, length), 0) < lax.broadcasted_iota(
        jnp.int32, (length, length), 1
    )
    rank = jnp.dot(
        jnp.broadcast_to(flat, (16, length)).astype(BF16),
        jnp.where(before, 1.0, 0.0).astype(BF16),
        preferred_element_type=F32,
    )[0:1]
    slot = jnp.where(flat > 0.0, rank, -1.0)
    lanes = lax.broadcasted_iota(jnp.int32, (window, size), 1).astype(F32)

    def chosen(row):
        column = jnp.broadcast_to(row, (LANES, window)).T[:, 0:1]
        return jnp.where(column == lanes, 1.0, 0.0)

    base = jnp.zeros((window, size), F32)
    for head in range(heads):
        own = slot[:, head * window : (head + 1) * window]
        pick = chosen(own).astype(BF16)
        for g in range(4):
            spot = jnp.where(core == g % 2, 0, 2) + g // 2
            pick_ref[head, pl.ds(pl.multiple_of(spot * block, block), block), :] = pick[
                g * block : (g + 1) * block
            ]
        earlier = jnp.full(own.shape, -1.0, F32)
        for k in range(1, 5):
            moved = jnp.concatenate([jnp.full((1, k), -1.0, F32), own[:, : window - k]], axis=1)
            earlier = jnp.where(offsets_ref[head] == k, moved, earlier)
        base = base + chosen(earlier)
    base = base.astype(BF16)
    for g in range(4):
        spot = jnp.where(core == g % 2, 0, 2) + jnp.where(zh == g // 2, 0, 1)
        base_ref[pl.ds(pl.multiple_of(spot * block, block), block), :] = base[g * block : (g + 1) * block]


def packed_rows(info, offsets, doc_ids, size):
    heads, window = offsets.shape[0], doc_ids.shape[0]
    ids = doc_ids.reshape(1, window)
    return pl.pallas_call(
        rows_kernel,
        in_specs=[SMEM, SMEM, whole(ids)],
        out_specs=[
            pl.BlockSpec((heads, window, size), lambda *_: (0, 0, 0)),
            pl.BlockSpec((window, size), lambda *_: (0, 0)),
            SMEM,
        ],
        out_shape=[
            jax.ShapeDtypeStruct((heads, window, size), BF16),
            jax.ShapeDtypeStruct((window, size), BF16),
            jax.ShapeDtypeStruct((1,), jnp.int32),
        ],
        compiler_params=params(),
        name="packed_rows",
    )(info, offsets, ids)


def shards(hidden, base_logits, doc_ids, offsets, block_weight, block_bias, projection):
    heads, depth, cols = block_weight.shape
    window = doc_ids.shape[0]
    rows, width = hidden.shape
    zh, core, y, x, zl = [lax.axis_index(a) for a in AXES]
    stretch_index = lax.axis_index(AXES)
    place = places(core, y, x, stretch_index, width // cols)
    z_shift = (zh * 2 + zl).reshape(1).astype(jnp.int32)
    no_shift = jnp.zeros((1,), jnp.int32)

    weight = block_weight.transpose(0, 2, 1).reshape(heads * cols, depth)
    proj = projection.T

    info = jnp.stack([core, zh]).astype(jnp.int32)

    def run(size, hidden, base_logits, doc_ids, offsets, proj, weight):
        plane = gather_plane(hidden, z_shift, no_shift)
        own_hidden = {0: plane, **{r: fetch(plane, 3, r) for r in (1, 3)}}
        other_hidden = {0: swap_core(plane)}
        kept, left = split_columns(zh.reshape(1), [after(base_logits, plane)])
        came = lax.ppermute(left, "zh", [(0, 1), (1, 0)])

        pick, pick_base, count = packed_rows(info, offsets, doc_ids, size)

        own_hidden[2] = fetch(plane, 3, 2)
        for r in (1, 3, 2):
            own_hidden[r] = after(own_hidden[r], pick, came, place)
            other_hidden[r] = swap_core(own_hidden[r])
        pre, packed = packed_states(place, own_hidden, other_hidden, weight, block_bias, pick)

        plane = gather_plane(packed, z_shift, no_shift)
        own = {0: plane, **{r: fetch(plane, 3, r) for r in (1, 3, 2)}}
        other = {0: swap_core(plane)}
        kept, left = split_columns(core.reshape(1), [after(kept, plane), came])
        far = swap_core(left)
        proj_turned = turned(after(proj, left))
        target = target_rows(after(kept, proj_turned), far, pick_base)
        logits = add_logits(place, after(proj, target), 0, [own[0], other[0]])[0]
        for r in (1, 3, 2):
            own[r] = after(own[r], logits)
            other[r] = swap_core(own[r])
        logits = add_logits(place, proj, 2, [own[r] for r in (1, 3, 2)], logits)[0]
        logits, stats = add_logits(place, proj, 5, [other[r] for r in (1, 3, 2)], logits, target)
        grad, loss = logits_grad(stats, logits, target, count)

        def piece(row, gate, *add):
            return state_grad_piece(place, proj_turned, row, after(grad, *gate), *add)

        there = {r: piece(OTHER[r], ()) for r in (2, 1)}
        sent = {r: swap_core(there[r]) for r in (2, 1)}
        here = {r: piece(OWN[r], (), sent[r]) for r in (2, 1)}
        for r in (3, 0):
            there[r] = piece(OTHER[r], (here[1],))
            sent[r] = swap_core(there[r])
        for r in (3, 0):
            here[r] = piece(OWN[r], (), sent[r])
        parts = [here[0]] + [fetch(here[r], 3, 4 - r) for r in (2, 1, 3)]
        grad_proj = projection_grad(
            place,
            after(grad, here[0]),
            depth,
            (0, 1, 2, 3, 4),
            [own[0], other[0], own[1], own[3], own[2]],
        )
        parts = sum_cut(no_shift, [after(p, grad_proj) for p in parts])
        moved = [fetch(parts[r], 2, 4 - r) for r in (1, 3, 2)]
        grad_proj = projection_grad(
            place,
            after(grad, parts[0]),
            depth,
            (5, 6, 7),
            [other[1], other[3], other[2]],
            grad_proj,
        )
        parts = sum_cut(z_shift, [parts[0]] + [after(m, grad_proj) for m in moved])
        sums = [parts[0]] + [fetch(parts[r], 1, 4 - r) for r in (1, 3, 2)]
        grad_block, grad_bias = block_grad(place, sums, pick, pre, own_hidden, other_hidden, depth)
        return grad_proj, grad_block, grad_bias, loss.reshape(()), count

    args = (hidden, base_logits, doc_ids, offsets, proj, weight)
    packed_size = 384
    *result, count = run(packed_size, *args)
    grad_proj, grad_block, grad_bias, loss = lax.cond(
        count[0] <= packed_size,
        lambda done, args: done,
        lambda done, args: run(heads * window, *args)[:4],
        tuple(result),
        args,
    )
    return (
        grad_proj.T,
        grad_block.reshape(heads, cols, depth).transpose(0, 2, 1),
        grad_bias,
        loss,
    )


def solution(mesh):
    fine = Mesh(mesh.devices.reshape(2, 2, 4, 4, 2), AXES)
    return jax.shard_map(
        shards,
        mesh=fine,
        in_specs=(
            P(SEQ, VOCAB),
            P(SEQ, VOCAB),
            P(),
            P(),
            P(None, None, SEQ + VOCAB),
            P(None, SEQ + VOCAB),
            P(None, VOCAB + SEQ),
        ),
        out_specs=(
            P(None, VOCAB + SEQ),
            P(None, None, SEQ + VOCAB),
            P(None, SEQ + VOCAB),
            P(),
        ),
        check_vma=False,
    )
```

```python
import functools

import jax
import jax.numpy as jnp
from jax import lax
from jax.experimental import pallas as pl
from jax.experimental.pallas import tpu as pltpu
from jax.sharding import Mesh, PartitionSpec as P

AXES = ("zh", "core", "y", "x", "zl")
CHIPS = ("zh", "y", "x", "zl")
SEQ = ("zh", "core")
VOCAB = ("y", "x", "zl")
BF16 = jnp.bfloat16
F32 = jnp.float32
VMEM_LIMIT = 18 * 1024 * 1024
LANES = 128
OWN = {0: 0, 1: 2, 3: 3, 2: 4}
OTHER = {0: 1, 1: 5, 3: 6, 2: 7}
NT = (((1,), (1,)), ((), ()))


def swap_core(x):
    return lax.ppermute(x, "core", [(0, 1), (1, 0)])


def fetch(value, stage, r):
    pairs = []
    for device in range(128):
        zh, core, y, x, zl = device // 64, device // 32 % 2, device // 8 % 4, device // 2 % 4, device % 2
        if stage == 1:
            z = (zh * 2 + zl + r) % 4
            zh, zl = z // 2, z % 2
        elif (stage == 2) == (core == 0):
            x = (x + r) % 4
        else:
            y = (y + r) % 4
        pairs.append((zh * 64 + core * 32 + y * 8 + x * 2 + zl, device))
    return lax.ppermute(value, AXES, pairs)


def params(limit=VMEM_LIMIT):
    return pltpu.CompilerParams(vmem_limit_bytes=limit)


def after(value, *earlier):
    return lax.optimization_barrier((value,) + earlier)[0]


SMEM = pl.BlockSpec(memory_space=pltpu.SMEM)
SMALL = pl.CostEstimate(flops=1, bytes_accessed=1, transcendentals=0)


def whole(array):
    return pl.BlockSpec(array.shape, lambda *_: (0,) * len(array.shape))


def join_kernel(shift_ref, a_ref, b_ref, c_ref, d_ref, out_ref):
    rows = a_ref.shape[0]
    for r, ref in enumerate((a_ref, b_ref, c_ref, d_ref)):
        place = lax.rem(shift_ref[0] + r, 4) * rows
        out_ref[pl.ds(pl.multiple_of(place, rows), rows), :] = ref[...]


def join(shift, parts):
    rows, size = parts[0].shape
    return pl.pallas_call(
        join_kernel,
        in_specs=[SMEM] + [whole(p) for p in parts],
        out_shape=jax.ShapeDtypeStruct((4 * rows, size), parts[0].dtype),
        compiler_params=params(),
        name="join",
    )(shift, *parts)


def sum_cut_kernel(shift_ref, *refs):
    parts, out_refs = refs[:-4], refs[-4:]
    rows = out_refs[0].shape[0]
    for r, out_ref in enumerate(out_refs):
        place = pl.ds(pl.multiple_of(lax.rem(shift_ref[0] + r, 4) * rows, rows), rows)
        total = parts[0][place, :].astype(F32)
        for part in parts[1:]:
            total += part[place, :].astype(F32)
        out_ref[...] = total.astype(BF16)


def sum_cut(shift, parts):
    rows, size = parts[0].shape
    return pl.pallas_call(
        sum_cut_kernel,
        in_specs=[SMEM] + [whole(p) for p in parts],
        out_shape=[jax.ShapeDtypeStruct((rows // 4, size), BF16)] * 4,
        compiler_params=params(),
        name="sum_cut",
    )(shift, *parts)


def gather_plane(chunk, z_shift, no_shift):
    line = join(z_shift, [chunk] + [fetch(chunk, 1, r) for r in (1, 2, 3)])
    return join(no_shift, [line] + [fetch(line, 2, r) for r in (1, 2, 3)])


def split_kernel(keep_ref, *refs):
    ins, kept_ref, left_ref = refs[:-2], refs[-2], refs[-1]
    rows, half = ins[0].shape[0], kept_ref.shape[1]
    second = keep_ref[0] == 1
    for index, ref in enumerate(ins):
        a, b = ref[:, :half], ref[:, half:]
        place = slice(index * rows, (index + 1) * rows)
        kept_ref[place, :] = jnp.where(second, b, a)
        left_ref[place, :] = jnp.where(second, a, b)


def split_columns(keep, parts):
    rows, size = parts[0].shape
    return pl.pallas_call(
        split_kernel,
        in_specs=[SMEM] + [whole(p) for p in parts],
        out_shape=[jax.ShapeDtypeStruct((len(parts) * rows, size // 2), F32)] * 2,
        compiler_params=params(),
        name="split_columns",
    )(keep, *parts)


def target_kernel(near_ref, far_ref, pick_ref, out_ref):
    half = near_ref.shape[0]
    total = None
    pieces = []
    for index, ref in enumerate((near_ref, far_ref)):
        pick = pick_ref[index * half : (index + 1) * half, :]
        value = ref[...]
        high = value.astype(BF16)
        rest = value - high.astype(F32)
        middle = rest.astype(BF16)
        low = (rest - middle.astype(F32)).astype(BF16)
        pieces.append((low, middle, high, pick))
    for part in range(3):
        for entry in pieces:
            more = lax.dot_general(
                entry[part], entry[3], (((0,), (0,)), ((), ())), preferred_element_type=F32
            )
            total = more if total is None else total + more
    out_ref[...] = total


def target_rows(near, far, pick):
    return pl.pallas_call(
        target_kernel,
        out_shape=jax.ShapeDtypeStruct((near.shape[1], pick.shape[1]), F32),
        compiler_params=params(),
        name="target_rows",
    )(near, far, pick)


def hidden_block(own_ref, other_ref, i, j, zl, rows):
    def part(ref, at, zh):
        start = (at * 4 + zh * 2 + zl) * rows
        return ref[start : start + rows, :]

    return jnp.concatenate(
        [part(own_ref, j, 0), part(own_ref, j, 1), part(other_ref, i, 0), part(other_ref, i, 1)], axis=0
    )


def states_kernel(place_ref, *refs):
    own_refs, other_refs = refs[:4], refs[4:8]
    weight_ref, bias_ref, pick_ref, pre_ref, packed_ref, near_ref = refs[8:]
    width = own_refs[0].shape[1]
    rows = own_refs[0].shape[0] // 16
    cols = packed_ref.shape[0]
    total = jnp.zeros(pre_ref.shape[::-1], F32)
    for i in range(4):
        for j in range(4):
            where = place_ref[64 + i * 4 + j]
            part = weight_ref[:, pl.ds(pl.multiple_of(where * 2 * width, 2 * width), 2 * width)]
            for zl in range(2):
                block = hidden_block(own_refs[i], other_refs[j], i, j, zl, rows)
                total += lax.dot_general(
                    block, part[:, zl * width : (zl + 1) * width], NT, preferred_element_type=F32
                )

    for i in range(4):
        for j in range(4):

            @pl.when(place_ref[64 + i * 4 + j] == place_ref[80] // 2)
            def _(i=i, j=j):
                for at, (ref, spot) in enumerate([(own_refs[i], j)] * 2 + [(other_refs[j], i)] * 2):
                    start = (spot * 4 + at % 2 * 2 + lax.rem(place_ref[80], 2)) * rows
                    near_ref[at * rows : (at + 1) * rows, :] = ref[pl.ds(pl.multiple_of(start, rows), rows), :]

    lane = lax.broadcasted_iota(jnp.int32, (cols, width), 1)
    row = lax.broadcasted_iota(jnp.int32, (cols, width), 0)
    select = (lane == row + place_ref[81] * cols).astype(BF16)
    own_cols = lax.dot_general(select, near_ref[...], NT, preferred_element_type=F32)

    bias = jnp.concatenate([bias_ref[head : head + 1, :] for head in range(pick_ref.shape[0])], axis=1)
    pre = (total + bias).T
    pre_ref[...] = pre
    packed = jnp.zeros(packed_ref.shape, F32)
    for head in range(pick_ref.shape[0]):
        own = pre[head * cols : (head + 1) * cols]
        state = (own_cols + own / (1.0 + jnp.exp(-own))).astype(BF16)
        packed += jnp.dot(state, pick_ref[head], preferred_element_type=F32)
    packed_ref[...] = packed.astype(BF16)


def packed_states(place, own, other, weight, bias, pick):
    heads, window, size = pick.shape
    cols = weight.shape[0] // heads
    args = [own[i] for i in range(4)] + [other[i] for i in range(4)] + [weight, bias, pick]
    return pl.pallas_call(
        states_kernel,
        in_specs=[SMEM] + [whole(a) for a in args],
        out_shape=[
            jax.ShapeDtypeStruct((heads * cols, window), F32),
            jax.ShapeDtypeStruct((cols, size), BF16),
        ],
        scratch_shapes=[pltpu.VMEM((window, own[0].shape[1]), BF16)],
        compiler_params=params(),
        name="packed_states",
    )(place, *args)


def logits_kernel(row, first, last, count, place_ref, proj_ref, *refs):
    pieces, rest = refs[:count], refs[count:]
    total = None
    if not first:
        total, rest = rest[0][...], rest[1:]
    if last:
        target_ref, rest = rest[0], rest[1:]
    at = row * 8
    for piece in pieces:
        blocks = piece.shape[0] // LANES
        proj = jnp.concatenate(
            [
                proj_ref[:, pl.ds(pl.multiple_of(place_ref[at + k] * LANES, LANES), LANES)]
                for k in range(blocks)
            ],
            axis=1,
        )
        at += blocks
        more = jnp.dot(proj, piece[...], preferred_element_type=F32)
        total = more if total is None else total + more
    rest[0][...] = total
    if last:
        logits = total
        target = target_ref[...]
        top_head = jnp.max(logits, axis=0, keepdims=True)
        top_base = jnp.max(target, axis=0, keepdims=True)
        exp_base = jnp.exp(target - top_base)
        sum_head = jnp.sum(jnp.exp(logits - top_head), axis=0, keepdims=True)
        sum_base = jnp.sum(exp_base, axis=0, keepdims=True)
        cross = jnp.sum(exp_base * (target - logits), axis=0, keepdims=True)
        rest[1][...] = jnp.concatenate(
            [top_head, sum_head, top_base, sum_base, cross, jnp.zeros((3, cross.shape[1]), F32)], 0
        )


def add_logits(place, proj, row, pieces, before=None, target=None):
    stretch = proj.shape[0]
    size = pieces[0].shape[1]
    count = len(pieces)
    args = [proj] + list(pieces) + ([] if before is None else [before]) + ([] if target is None else [target])
    out_shape = [jax.ShapeDtypeStruct((stretch, size), F32)]
    if target is not None:
        out_shape.append(jax.ShapeDtypeStruct((8, size), F32))
    return pl.pallas_call(
        functools.partial(logits_kernel, row, before is None, target is not None, count),
        in_specs=[SMEM] + [whole(a) for a in args],
        out_shape=out_shape,
        compiler_params=params(),
        cost_estimate=SMALL,
        name="add_logits",
    )(place, *args)


def pair_kernel(a_ref, b_ref, out_ref):
    size = a_ref.shape[1]
    a, b = a_ref[...], b_ref[...]
    top_head = jnp.maximum(a[0:1], b[0:1])
    top_base = jnp.maximum(a[2:3], b[2:3])
    ah, bh = jnp.exp(a[0:1] - top_head), jnp.exp(b[0:1] - top_head)
    ab, bb = jnp.exp(a[2:3] - top_base), jnp.exp(b[2:3] - top_base)
    merged = (
        top_head,
        a[1:2] * ah + b[1:2] * bh,
        top_base,
        a[3:4] * ab + b[3:4] * bb,
        a[4:5] * ab + b[4:5] * bb,
    )
    groups = size // LANES
    rows = [m[:, g * LANES : (g + 1) * LANES] for m in merged for g in range(groups)]
    pad = out_ref.shape[1] - len(rows)
    packed = jnp.concatenate(rows + [jnp.zeros((pad, LANES), F32)], axis=0)
    for index in range(out_ref.shape[0]):
        out_ref[index] = packed


def finish_kernel(count_ref, parts_ref, logits_ref, target_ref, grad_ref, loss_ref):
    size = logits_ref.shape[1]
    groups = size // LANES
    parts = parts_ref[...]

    def rows(k):
        return parts[:, k * groups : (k + 1) * groups, :]

    def flat(value):
        return jnp.concatenate([value[g : g + 1, :] for g in range(groups)], axis=1)

    top_head = jnp.max(rows(0), axis=0)
    top_base = jnp.max(rows(2), axis=0)
    head = jnp.exp(rows(0) - top_head[None])
    base = jnp.exp(rows(2) - top_base[None])
    sum_head = flat(jnp.sum(rows(1) * head, axis=0))
    sum_base = flat(jnp.sum(rows(3) * base, axis=0))
    cross = flat(jnp.sum(rows(4) * base, axis=0))
    top_head, top_base = flat(top_head), flat(top_base)
    mask = lax.broadcasted_iota(jnp.int32, (1, size), 1) < count_ref[0]
    kl = cross / sum_base - (top_base + jnp.log(sum_base)) + (top_head + jnp.log(sum_head))
    total = jnp.sum(jnp.where(mask, kl, 0.0), axis=1, keepdims=True)
    loss_ref[...] = total / jnp.maximum(count_ref[0].astype(F32), 1.0)
    keep = mask.astype(F32)
    grad_ref[...] = (
        keep
        * (
            jnp.exp(logits_ref[...] - top_head) * (1.0 / sum_head)
            - jnp.exp(target_ref[...] - top_base) * (1.0 / sum_base)
        )
    ).astype(BF16)


def logits_grad(stats, logits, target, count):
    size = stats.shape[1]
    rows = -(-5 * (size // LANES) // 8) * 8
    packed = pl.pallas_call(
        pair_kernel,
        out_shape=jax.ShapeDtypeStruct((64, rows, LANES), F32),
        compiler_params=params(),
        name="merge_pair",
    )(stats, swap_core(stats))
    parts = lax.all_to_all(packed, CHIPS, split_axis=0, concat_axis=0, tiled=True)
    args = [parts, logits, target]
    return pl.pallas_call(
        finish_kernel,
        in_specs=[SMEM] + [whole(a) for a in args],
        out_shape=[
            jax.ShapeDtypeStruct(logits.shape, BF16),
            jax.ShapeDtypeStruct((1, 1), F32),
        ],
        compiler_params=params(),
        name="logits_grad",
    )(count, *args)


def state_grad_kernel(row, place_ref, proj_ref, grad_ref, *refs):
    blocks = [
        proj_ref[:, pl.ds(pl.multiple_of(place_ref[row * 8 + k] * LANES, LANES), LANES)] for k in range(8)
    ]
    total = lax.dot_general(
        jnp.concatenate(blocks, axis=1),
        grad_ref[...],
        (((0,), (0,)), ((), ())),
        preferred_element_type=F32,
    )
    if len(refs) == 2:
        total = total + refs[0][...].astype(F32)
    refs[-1][...] = total.astype(BF16)


def state_grad_piece(place, proj, row, grad, add=None):
    size = grad.shape[1]
    args = [proj, grad] + ([] if add is None else [add])
    return pl.pallas_call(
        functools.partial(state_grad_kernel, row),
        in_specs=[SMEM] + [whole(a) for a in args],
        out_shape=jax.ShapeDtypeStruct((8 * LANES, size), BF16),
        compiler_params=params(),
        cost_estimate=SMALL,
        name="state_grad_piece",
    )(place, *args)


def grad_proj_kernel(starts, place_ref, grad_ref, *refs):
    pieces, (out_ref, slots_ref, sem) = refs[: len(starts)], refs[-3:]
    blocks = [piece.shape[0] // LANES for piece in pieces]

    def copy(step, k):
        place = pl.multiple_of(place_ref[starts[step] + k] * LANES, LANES)
        return pltpu.make_async_copy(
            slots_ref.at[step % 2, :, pl.ds(k * LANES, LANES)],
            out_ref.at[:, pl.ds(place, LANES)],
            sem.at[step % 2, k],
        )

    for step, piece in enumerate(pieces):
        if step >= 2:
            for k in range(blocks[step - 2]):
                copy(step - 2, k).wait()
        slots_ref[step % 2, :, : piece.shape[0]] = lax.dot_general(
            grad_ref[...], piece[...], NT, preferred_element_type=F32
        ).astype(BF16)
        for k in range(blocks[step]):
            copy(step, k).start()
    for step in range(max(len(starts) - 2, 0), len(starts)):
        for k in range(blocks[step]):
            copy(step, k).wait()


def projection_grad(place, grad, depth, starts, pieces, before=None):
    stretch, size = grad.shape
    height = pieces[0].shape[0]
    anywhere = pl.BlockSpec(memory_space=pltpu.HBM)
    more = [] if before is None else [before]
    return pl.pallas_call(
        functools.partial(grad_proj_kernel, starts),
        in_specs=[SMEM, whole(grad)] + [whole(p) for p in pieces] + [anywhere] * len(more),
        out_specs=anywhere,
        out_shape=jax.ShapeDtypeStruct((stretch, depth), BF16),
        scratch_shapes=[pltpu.VMEM((2, stretch, height), BF16), pltpu.SemaphoreType.DMA((2, 8))],
        input_output_aliases={} if before is None else {2 + len(pieces): 0},
        compiler_params=params(),
        cost_estimate=SMALL,
        name="projection_grad",
    )(place, grad, *pieces, *more)


def grad_block_kernel(place_ref, *refs):
    sums, pick_ref, pre_ref, own_refs, other_refs = refs[:4], refs[4], refs[5], refs[6:10], refs[10:14]
    out_ref, bias_ref, pre_grad_ref = refs[14:]
    width = own_refs[0].shape[1]
    rows = own_refs[0].shape[0] // 16
    cols = sums[0].shape[0]
    total = sums[0][...].astype(F32) + sums[1][...].astype(F32)
    total = total + (sums[2][...].astype(F32) + sums[3][...].astype(F32))
    high = total.astype(BF16)
    rest = total - high.astype(F32)
    middle = rest.astype(BF16)
    low = (rest - middle.astype(F32)).astype(BF16)
    for head in range(pick_ref.shape[0]):
        own = slice(head * cols, (head + 1) * cols)
        spread = sum(
            lax.dot_general(piece, pick_ref[head], NT, preferred_element_type=F32)
            for piece in (low, middle, high)
        )
        pre = pre_ref[own]
        sigma = 1.0 / (1.0 + jnp.exp(-pre))
        pre_grad = spread * (sigma * (1.0 + pre * (1.0 - sigma)))
        bias_ref[head : head + 1, :] = jnp.sum(pre_grad.T, axis=0, keepdims=True)
        pre_grad_ref[own] = pre_grad.astype(BF16)
    grad = pre_grad_ref[...]
    for i in range(4):
        for j in range(4):
            halves = [
                jnp.dot(
                    grad,
                    hidden_block(own_refs[i], other_refs[j], i, j, zl, rows),
                    preferred_element_type=F32,
                ).astype(BF16)
                for zl in range(2)
            ]
            place = pl.multiple_of(place_ref[64 + i * 4 + j] * 2 * width, 2 * width)
            out_ref[:, pl.ds(place, 2 * width)] = jnp.concatenate(halves, axis=1)


def block_grad(place, sums, pick, pre, own, other, depth):
    heads, window, size = pick.shape
    cols = sums[0].shape[0]
    args = list(sums) + [pick, pre] + [own[i] for i in range(4)] + [other[i] for i in range(4)]
    return pl.pallas_call(
        grad_block_kernel,
        in_specs=[SMEM] + [whole(a) for a in args],
        out_shape=[
            jax.ShapeDtypeStruct((heads * cols, depth), BF16),
            jax.ShapeDtypeStruct((heads, cols), F32),
        ],
        scratch_shapes=[pltpu.VMEM((heads * cols, window), BF16)],
        compiler_params=params(),
        name="block_grad",
    )(place, *args)


def place_kernel(share, info_ref, out_ref):
    core, y, x, stretch = [info_ref[k] for k in range(4)]
    for table, which in ((OWN, core), (OTHER, 1 - core)):
        for third in range(4):
            for second in range(4):
                y_at = lax.rem(y + jnp.where(which == 0, third, second), 4)
                x_at = lax.rem(x + jnp.where(which == 0, second, third), 4)
                plane = y_at * 4 + x_at
                for zh in range(2):
                    out_ref[table[third] * 8 + second * 2 + zh] = zh * 32 + which * 16 + plane
                if table is OWN:
                    out_ref[64 + third * 4 + second] = plane
    out_ref[80] = stretch // share
    out_ref[81] = lax.rem(stretch, share)


def places(core, y, x, stretch_index, share):
    return pl.pallas_call(
        functools.partial(place_kernel, share),
        in_specs=[SMEM],
        out_specs=SMEM,
        out_shape=jax.ShapeDtypeStruct((82,), jnp.int32),
        name="places",
    )(jnp.stack([core, y, x, stretch_index]).astype(jnp.int32))


def rows_kernel(info_ref, offsets_ref, ids_ref, pick_ref, base_ref, count_ref):
    heads, window, size = pick_ref.shape
    core, zh = info_ref[0], info_ref[1]
    block = window // 4
    ids = ids_ref[...]
    valid = []
    for head in range(heads):
        later = jnp.full(ids.shape, -1, jnp.int32)
        for k in range(1, 5):
            moved = jnp.concatenate([ids[:, k:], jnp.full((1, k), -1, jnp.int32)], axis=1)
            later = jnp.where(offsets_ref[head] == k, moved, later)
        valid.append(jnp.where(later == ids, 1.0, 0.0))
    flat = jnp.concatenate(valid, axis=1)
    count_ref[0] = jnp.sum(flat).astype(jnp.int32)
    length = heads * window
    before = lax.broadcasted_iota(jnp.int32, (length, length), 0) < lax.broadcasted_iota(
        jnp.int32, (length, length), 1
    )
    rank = jnp.dot(
        jnp.broadcast_to(flat, (16, length)).astype(BF16),
        jnp.where(before, 1.0, 0.0).astype(BF16),
        preferred_element_type=F32,
    )[0:1]
    slot = jnp.where(flat > 0.0, rank, -1.0)
    lanes = lax.broadcasted_iota(jnp.int32, (window, size), 1).astype(F32)

    def chosen(row):
        column = jnp.broadcast_to(row, (LANES, window)).T[:, 0:1]
        return jnp.where(column == lanes, 1.0, 0.0)

    base = jnp.zeros((window, size), F32)
    for head in range(heads):
        own = slot[:, head * window : (head + 1) * window]
        pick = chosen(own).astype(BF16)
        for g in range(4):
            spot = jnp.where(core == g % 2, 0, 2) + g // 2
            pick_ref[head, pl.ds(pl.multiple_of(spot * block, block), block), :] = pick[
                g * block : (g + 1) * block
            ]
        earlier = jnp.full(own.shape, -1.0, F32)
        for k in range(1, 5):
            moved = jnp.concatenate([jnp.full((1, k), -1.0, F32), own[:, : window - k]], axis=1)
            earlier = jnp.where(offsets_ref[head] == k, moved, earlier)
        base = base + chosen(earlier)
    base = base.astype(BF16)
    for g in range(4):
        spot = jnp.where(core == g % 2, 0, 2) + jnp.where(zh == g // 2, 0, 1)
        base_ref[pl.ds(pl.multiple_of(spot * block, block), block), :] = base[g * block : (g + 1) * block]


def packed_rows(info, offsets, doc_ids, size):
    heads, window = offsets.shape[0], doc_ids.shape[0]
    ids = doc_ids.reshape(1, window)
    return pl.pallas_call(
        rows_kernel,
        in_specs=[SMEM, SMEM, whole(ids)],
        out_specs=[
            pl.BlockSpec((heads, window, size), lambda *_: (0, 0, 0)),
            pl.BlockSpec((window, size), lambda *_: (0, 0)),
            SMEM,
        ],
        out_shape=[
            jax.ShapeDtypeStruct((heads, window, size), BF16),
            jax.ShapeDtypeStruct((window, size), BF16),
            jax.ShapeDtypeStruct((1,), jnp.int32),
        ],
        compiler_params=params(),
        name="packed_rows",
    )(info, offsets, ids)


def shards(hidden, base_logits, doc_ids, offsets, block_weight, block_bias, projection):
    heads, depth, cols = block_weight.shape
    window = doc_ids.shape[0]
    rows, width = hidden.shape
    zh, core, y, x, zl = [lax.axis_index(a) for a in AXES]
    stretch_index = lax.axis_index(AXES)
    place = places(core, y, x, stretch_index, width // cols)
    z_shift = (zh * 2 + zl).reshape(1).astype(jnp.int32)
    no_shift = jnp.zeros((1,), jnp.int32)

    weight = block_weight.transpose(0, 2, 1).reshape(heads * cols, depth)
    proj = projection.T

    info = jnp.stack([core, zh]).astype(jnp.int32)

    def run(size, hidden, base_logits, doc_ids, offsets, proj, weight):
        plane = gather_plane(hidden, z_shift, no_shift)
        own_hidden = {0: plane, **{r: fetch(plane, 3, r) for r in (1, 3)}}
        kept, left = split_columns(zh.reshape(1), [after(base_logits, plane)])
        came = lax.ppermute(left, "zh", [(0, 1), (1, 0)])

        pick, pick_base, count = packed_rows(info, offsets, doc_ids, size)

        own_hidden[2] = fetch(plane, 3, 2)
        other_hidden = {0: swap_core(plane)}
        for r in (1, 3, 2):
            own_hidden[r] = after(own_hidden[r], pick, came, place)
            other_hidden[r] = swap_core(own_hidden[r])
        pre, packed = packed_states(place, own_hidden, other_hidden, weight, block_bias, pick)

        plane = gather_plane(packed, z_shift, no_shift)
        own = {0: plane, **{r: fetch(plane, 3, r) for r in (1, 3)}}
        other = {0: swap_core(plane)}
        kept, left = split_columns(core.reshape(1), [after(kept, plane), came])
        far = swap_core(left)
        target = target_rows(kept, far, pick_base)
        logits = add_logits(place, after(proj, target), 0, [own[0], other[0]])[0]
        half = plane.shape[0] // 2
        for r in (1, 3):
            own[r] = after(own[r], logits)
        far_own = [fetch(own[1][:half], 3, 1), fetch(own[3][half:], 3, 3)]
        for r in (1, 3):
            other[r] = swap_core(own[r])
        logits = add_logits(place, proj, 2, [own[r] for r in (1, 3)], logits)[0]
        logits = add_logits(place, proj, 5, [other[r] for r in (1, 3)], logits)[0]
        far_own = [after(v, logits) for v in far_own]
        far_other = [swap_core(v) for v in far_own]
        logits = add_logits(place, proj, 4, far_own, logits)[0]
        logits, stats = add_logits(place, proj, 7, far_other, logits, target)
        grad, loss = logits_grad(stats, logits, target, count)

        def piece(row, gates=(), add=None):
            return state_grad_piece(place, proj, row, after(grad, *gates), add)

        there = {r: piece(OTHER[r]) for r in (2, 1)}
        sent = {r: swap_core(there[r]) for r in (2, 1)}
        here = {r: piece(OWN[r], (), sent[r]) for r in (2, 1)}
        for r in (3, 0):
            there[r] = piece(OTHER[r], (here[1],))
            sent[r] = swap_core(there[r])
        for r in (3, 0):
            here[r] = piece(OWN[r], (), sent[r])
        parts = [here[0]] + [fetch(here[r], 3, 4 - r) for r in (2, 1, 3)]
        grad_proj = projection_grad(
            place,
            after(grad, here[0]),
            depth,
            (0, 8, 16, 24, 40, 48),
            [own[0], other[0], own[1], own[3], other[1], other[3]],
        )
        parts = sum_cut(no_shift, [after(p, grad_proj) for p in parts])
        moved = [fetch(parts[r], 2, 4 - r) for r in (1, 3, 2)]
        grad_proj = projection_grad(
            place,
            after(grad, parts[0]),
            depth,
            (32, 36, 56, 60),
            far_own + far_other,
            grad_proj,
        )
        parts = sum_cut(z_shift, [parts[0]] + [after(m, grad_proj) for m in moved])
        sums = [parts[0]] + [fetch(parts[r], 1, 4 - r) for r in (1, 3, 2)]
        grad_block, grad_bias = block_grad(place, sums, pick, pre, own_hidden, other_hidden, depth)
        return grad_proj, grad_block, grad_bias, loss.reshape(()), count

    args = (hidden, base_logits, doc_ids, offsets, proj, weight)
    packed_size = 384
    *result, count = run(packed_size, *args)
    grad_proj, grad_block, grad_bias, loss = lax.cond(
        count[0] <= packed_size,
        lambda done, args: done,
        lambda done, args: run(heads * window, *args)[:4],
        tuple(result),
        args,
    )
    return (
        grad_proj.T,
        grad_block.reshape(heads, cols, depth).transpose(0, 2, 1),
        grad_bias,
        loss,
    )


def solution(mesh):
    fine = Mesh(mesh.devices.reshape(2, 2, 4, 4, 2), AXES)
    return jax.shard_map(
        shards,
        mesh=fine,
        in_specs=(
            P(SEQ, VOCAB),
            P(SEQ, VOCAB),
            P(),
            P(),
            P(None, None, SEQ + VOCAB),
            P(None, SEQ + VOCAB),
            P(None, VOCAB + SEQ),
        ),
        out_specs=(
            P(None, VOCAB + SEQ),
            P(None, None, SEQ + VOCAB),
            P(None, SEQ + VOCAB),
            P(),
        ),
        check_vma=False,
    )
```

```python
import functools

import jax
import jax.numpy as jnp
from jax import lax
from jax.experimental import pallas as pl
from jax.experimental.pallas import tpu as pltpu
from jax.sharding import Mesh, PartitionSpec as P

AXES = ("zh", "core", "y", "x", "zl")
CHIPS = ("zh", "y", "x", "zl")
SEQ = ("zh", "core")
VOCAB = ("y", "x", "zl")
BF16 = jnp.bfloat16
F32 = jnp.float32
VMEM_LIMIT = 18 * 1024 * 1024
LANES = 128
OWN = {0: 0, 1: 2, 3: 3, 2: 4}
OTHER = {0: 1, 1: 5, 3: 6, 2: 7}
NT = (((1,), (1,)), ((), ()))


def swap_core(x):
    return lax.ppermute(x, "core", [(0, 1), (1, 0)])


def fetch(value, stage, r):
    pairs = []
    for device in range(128):
        zh, core, y, x, zl = device // 64, device // 32 % 2, device // 8 % 4, device // 2 % 4, device % 2
        if stage == 1:
            z = (zh * 2 + zl + r) % 4
            zh, zl = z // 2, z % 2
        elif (stage == 2) == (core == 0):
            x = (x + r) % 4
        else:
            y = (y + r) % 4
        pairs.append((zh * 64 + core * 32 + y * 8 + x * 2 + zl, device))
    return lax.ppermute(value, AXES, pairs)


def params(limit=VMEM_LIMIT):
    return pltpu.CompilerParams(vmem_limit_bytes=limit)


def after(value, *earlier):
    return lax.optimization_barrier((value,) + earlier)[0]


SMEM = pl.BlockSpec(memory_space=pltpu.SMEM)
SMALL = pl.CostEstimate(flops=1, bytes_accessed=1, transcendentals=0)


def whole(array):
    return pl.BlockSpec(array.shape, lambda *_: (0,) * len(array.shape))


def join_kernel(shift_ref, a_ref, b_ref, c_ref, d_ref, out_ref):
    rows = a_ref.shape[0]
    for r, ref in enumerate((a_ref, b_ref, c_ref, d_ref)):
        place = lax.rem(shift_ref[0] + r, 4) * rows
        out_ref[pl.ds(pl.multiple_of(place, rows), rows), :] = ref[...]


def join(shift, parts):
    rows, size = parts[0].shape
    return pl.pallas_call(
        join_kernel,
        in_specs=[SMEM] + [whole(p) for p in parts],
        out_shape=jax.ShapeDtypeStruct((4 * rows, size), parts[0].dtype),
        compiler_params=params(),
        name="join",
    )(shift, *parts)


def sum_cut_kernel(shift_ref, *refs):
    parts, out_refs = refs[:-4], refs[-4:]
    rows = out_refs[0].shape[0]
    for r, out_ref in enumerate(out_refs):
        place = pl.ds(pl.multiple_of(lax.rem(shift_ref[0] + r, 4) * rows, rows), rows)
        total = parts[0][place, :].astype(F32)
        for part in parts[1:]:
            total += part[place, :].astype(F32)
        out_ref[...] = total.astype(BF16)


def sum_cut(shift, parts):
    rows, size = parts[0].shape
    return pl.pallas_call(
        sum_cut_kernel,
        in_specs=[SMEM] + [whole(p) for p in parts],
        out_shape=[jax.ShapeDtypeStruct((rows // 4, size), BF16)] * 4,
        compiler_params=params(),
        name="sum_cut",
    )(shift, *parts)


def gather_plane(chunk, z_shift, no_shift):
    line = join(z_shift, [chunk] + [fetch(chunk, 1, r) for r in (1, 2, 3)])
    return join(no_shift, [line] + [fetch(line, 2, r) for r in (1, 2, 3)])


def split_kernel(keep_ref, *refs):
    ins, kept_ref, left_ref = refs[:-2], refs[-2], refs[-1]
    rows, half = ins[0].shape[0], kept_ref.shape[1]
    second = keep_ref[0] == 1
    for index, ref in enumerate(ins):
        a, b = ref[:, :half], ref[:, half:]
        place = slice(index * rows, (index + 1) * rows)
        kept_ref[place, :] = jnp.where(second, b, a)
        left_ref[place, :] = jnp.where(second, a, b)


def split_columns(keep, parts):
    rows, size = parts[0].shape
    return pl.pallas_call(
        split_kernel,
        in_specs=[SMEM] + [whole(p) for p in parts],
        out_shape=[jax.ShapeDtypeStruct((len(parts) * rows, size // 2), F32)] * 2,
        compiler_params=params(),
        name="split_columns",
    )(keep, *parts)


def target_kernel(near_ref, far_ref, pick_ref, out_ref):
    half = near_ref.shape[0]
    total = None
    pieces = []
    for index, ref in enumerate((near_ref, far_ref)):
        pick = pick_ref[index * half : (index + 1) * half, :]
        value = ref[...]
        high = value.astype(BF16)
        rest = value - high.astype(F32)
        middle = rest.astype(BF16)
        low = (rest - middle.astype(F32)).astype(BF16)
        pieces.append((low, middle, high, pick))
    for part in range(3):
        for entry in pieces:
            more = lax.dot_general(
                entry[part], entry[3], (((0,), (0,)), ((), ())), preferred_element_type=F32
            )
            total = more if total is None else total + more
    out_ref[...] = total


def target_rows(near, far, pick):
    return pl.pallas_call(
        target_kernel,
        out_shape=jax.ShapeDtypeStruct((near.shape[1], pick.shape[1]), F32),
        compiler_params=params(),
        name="target_rows",
    )(near, far, pick)


def hidden_block(own_ref, other_ref, i, j, zl, rows):
    def part(ref, at, zh):
        start = (at * 4 + zh * 2 + zl) * rows
        return ref[start : start + rows, :]

    return jnp.concatenate(
        [part(own_ref, j, 0), part(own_ref, j, 1), part(other_ref, i, 0), part(other_ref, i, 1)], axis=0
    )


def states_kernel(place_ref, *refs):
    own_refs, other_refs = refs[:4], refs[4:8]
    weight_ref, bias_ref, pick_ref, pre_ref, packed_ref, near_ref = refs[8:]
    width = own_refs[0].shape[1]
    rows = own_refs[0].shape[0] // 16
    cols = packed_ref.shape[0]
    total = jnp.zeros(pre_ref.shape[::-1], F32)
    for i in range(4):
        for j in range(4):
            where = place_ref[64 + i * 4 + j]
            part = weight_ref[:, pl.ds(pl.multiple_of(where * 2 * width, 2 * width), 2 * width)]
            for zl in range(2):
                block = hidden_block(own_refs[i], other_refs[j], i, j, zl, rows)
                total += lax.dot_general(
                    block, part[:, zl * width : (zl + 1) * width], NT, preferred_element_type=F32
                )

    for i in range(4):
        for j in range(4):

            @pl.when(place_ref[64 + i * 4 + j] == place_ref[80] // 2)
            def _(i=i, j=j):
                for at, (ref, spot) in enumerate([(own_refs[i], j)] * 2 + [(other_refs[j], i)] * 2):
                    start = (spot * 4 + at % 2 * 2 + lax.rem(place_ref[80], 2)) * rows
                    near_ref[at * rows : (at + 1) * rows, :] = ref[pl.ds(pl.multiple_of(start, rows), rows), :]

    lane = lax.broadcasted_iota(jnp.int32, (cols, width), 1)
    row = lax.broadcasted_iota(jnp.int32, (cols, width), 0)
    select = (lane == row + place_ref[81] * cols).astype(BF16)
    own_cols = lax.dot_general(select, near_ref[...], NT, preferred_element_type=F32)

    bias = jnp.concatenate([bias_ref[head : head + 1, :] for head in range(pick_ref.shape[0])], axis=1)
    pre = (total + bias).T
    pre_ref[...] = pre
    packed = jnp.zeros(packed_ref.shape, F32)
    for head in range(pick_ref.shape[0]):
        own = pre[head * cols : (head + 1) * cols]
        state = (own_cols + own / (1.0 + jnp.exp(-own))).astype(BF16)
        packed += jnp.dot(state, pick_ref[head], preferred_element_type=F32)
    packed_ref[...] = packed.astype(BF16)


def packed_states(place, own, other, weight, bias, pick):
    heads, window, size = pick.shape
    cols = weight.shape[0] // heads
    args = [own[i] for i in range(4)] + [other[i] for i in range(4)] + [weight, bias, pick]
    return pl.pallas_call(
        states_kernel,
        in_specs=[SMEM] + [whole(a) for a in args],
        out_shape=[
            jax.ShapeDtypeStruct((heads * cols, window), F32),
            jax.ShapeDtypeStruct((cols, size), BF16),
        ],
        scratch_shapes=[pltpu.VMEM((window, own[0].shape[1]), BF16)],
        compiler_params=params(),
        name="packed_states",
    )(place, *args)


def logits_kernel(row, first, last, count, place_ref, proj_ref, *refs):
    pieces, rest = refs[:count], refs[count:]
    total = None
    if not first:
        total, rest = rest[0][...], rest[1:]
    if last:
        target_ref, rest = rest[0], rest[1:]
    at = row * 8
    for piece in pieces:
        blocks = piece.shape[0] // LANES
        proj = jnp.concatenate(
            [
                proj_ref[:, pl.ds(pl.multiple_of(place_ref[at + k] * LANES, LANES), LANES)]
                for k in range(blocks)
            ],
            axis=1,
        )
        at += blocks
        more = jnp.dot(proj, piece[...], preferred_element_type=F32)
        total = more if total is None else total + more
    rest[0][...] = total
    if last:
        logits = total
        target = target_ref[...]
        top_head = jnp.max(logits, axis=0, keepdims=True)
        top_base = jnp.max(target, axis=0, keepdims=True)
        exp_base = jnp.exp(target - top_base)
        sum_head = jnp.sum(jnp.exp(logits - top_head), axis=0, keepdims=True)
        sum_base = jnp.sum(exp_base, axis=0, keepdims=True)
        cross = jnp.sum(exp_base * (target - logits), axis=0, keepdims=True)
        rest[1][...] = jnp.concatenate(
            [top_head, sum_head, top_base, sum_base, cross, jnp.zeros((3, cross.shape[1]), F32)], 0
        )


def add_logits(place, proj, row, pieces, before=None, target=None):
    stretch = proj.shape[0]
    size = pieces[0].shape[1]
    count = len(pieces)
    args = [proj] + list(pieces) + ([] if before is None else [before]) + ([] if target is None else [target])
    out_shape = [jax.ShapeDtypeStruct((stretch, size), F32)]
    if target is not None:
        out_shape.append(jax.ShapeDtypeStruct((8, size), F32))
    return pl.pallas_call(
        functools.partial(logits_kernel, row, before is None, target is not None, count),
        in_specs=[SMEM] + [whole(a) for a in args],
        out_shape=out_shape,
        compiler_params=params(),
        cost_estimate=SMALL,
        name="add_logits",
    )(place, *args)


def pair_kernel(a_ref, b_ref, out_ref):
    size = a_ref.shape[1]
    a, b = a_ref[...], b_ref[...]
    top_head = jnp.maximum(a[0:1], b[0:1])
    top_base = jnp.maximum(a[2:3], b[2:3])
    ah, bh = jnp.exp(a[0:1] - top_head), jnp.exp(b[0:1] - top_head)
    ab, bb = jnp.exp(a[2:3] - top_base), jnp.exp(b[2:3] - top_base)
    merged = (
        top_head,
        a[1:2] * ah + b[1:2] * bh,
        top_base,
        a[3:4] * ab + b[3:4] * bb,
        a[4:5] * ab + b[4:5] * bb,
    )
    groups = size // LANES
    rows = [m[:, g * LANES : (g + 1) * LANES] for m in merged for g in range(groups)]
    pad = out_ref.shape[1] - len(rows)
    packed = jnp.concatenate(rows + [jnp.zeros((pad, LANES), F32)], axis=0)
    for index in range(out_ref.shape[0]):
        out_ref[index] = packed


def finish_kernel(count_ref, parts_ref, logits_ref, target_ref, grad_ref, loss_ref):
    size = logits_ref.shape[1]
    groups = size // LANES
    parts = parts_ref[...]

    def rows(k):
        return parts[:, k * groups : (k + 1) * groups, :]

    def flat(value):
        return jnp.concatenate([value[g : g + 1, :] for g in range(groups)], axis=1)

    top_head = jnp.max(rows(0), axis=0)
    top_base = jnp.max(rows(2), axis=0)
    head = jnp.exp(rows(0) - top_head[None])
    base = jnp.exp(rows(2) - top_base[None])
    sum_head = flat(jnp.sum(rows(1) * head, axis=0))
    sum_base = flat(jnp.sum(rows(3) * base, axis=0))
    cross = flat(jnp.sum(rows(4) * base, axis=0))
    top_head, top_base = flat(top_head), flat(top_base)
    mask = lax.broadcasted_iota(jnp.int32, (1, size), 1) < count_ref[0]
    kl = cross / sum_base - (top_base + jnp.log(sum_base)) + (top_head + jnp.log(sum_head))
    total = jnp.sum(jnp.where(mask, kl, 0.0), axis=1, keepdims=True)
    loss_ref[...] = total / jnp.maximum(count_ref[0].astype(F32), 1.0)
    keep = mask.astype(F32)
    grad_ref[...] = (
        keep
        * (
            jnp.exp(logits_ref[...] - top_head) * (1.0 / sum_head)
            - jnp.exp(target_ref[...] - top_base) * (1.0 / sum_base)
        )
    ).astype(BF16)


def logits_grad(stats, logits, target, count):
    size = stats.shape[1]
    rows = -(-5 * (size // LANES) // 8) * 8
    packed = pl.pallas_call(
        pair_kernel,
        out_shape=jax.ShapeDtypeStruct((64, rows, LANES), F32),
        compiler_params=params(),
        name="merge_pair",
    )(stats, swap_core(stats))
    parts = lax.all_to_all(packed, CHIPS, split_axis=0, concat_axis=0, tiled=True)
    args = [parts, logits, target]
    return pl.pallas_call(
        finish_kernel,
        in_specs=[SMEM] + [whole(a) for a in args],
        out_shape=[
            jax.ShapeDtypeStruct(logits.shape, BF16),
            jax.ShapeDtypeStruct((1, 1), F32),
        ],
        compiler_params=params(),
        name="logits_grad",
    )(count, *args)


def state_grad_kernel(row, place_ref, proj_ref, grad_ref, *refs):
    blocks = [
        proj_ref[:, pl.ds(pl.multiple_of(place_ref[row * 8 + k] * LANES, LANES), LANES)] for k in range(8)
    ]
    total = lax.dot_general(
        jnp.concatenate(blocks, axis=1),
        grad_ref[...],
        (((0,), (0,)), ((), ())),
        preferred_element_type=F32,
    )
    if len(refs) == 2:
        total = total + refs[0][...].astype(F32)
    refs[-1][...] = total.astype(BF16)


def state_grad_piece(place, proj, row, grad, add=None):
    size = grad.shape[1]
    args = [proj, grad] + ([] if add is None else [add])
    return pl.pallas_call(
        functools.partial(state_grad_kernel, row),
        in_specs=[SMEM] + [whole(a) for a in args],
        out_shape=jax.ShapeDtypeStruct((8 * LANES, size), BF16),
        compiler_params=params(),
        cost_estimate=SMALL,
        name="state_grad_piece",
    )(place, *args)


def grad_proj_kernel(starts, place_ref, grad_ref, *refs):
    pieces, (out_ref, slots_ref, sem) = refs[: len(starts)], refs[-3:]
    blocks = [piece.shape[0] // LANES for piece in pieces]

    def copy(step, k):
        place = pl.multiple_of(place_ref[starts[step] + k] * LANES, LANES)
        return pltpu.make_async_copy(
            slots_ref.at[step % 2, :, pl.ds(k * LANES, LANES)],
            out_ref.at[:, pl.ds(place, LANES)],
            sem.at[step % 2, k],
        )

    for step, piece in enumerate(pieces):
        if step >= 2:
            for k in range(blocks[step - 2]):
                copy(step - 2, k).wait()
        slots_ref[step % 2, :, : piece.shape[0]] = lax.dot_general(
            grad_ref[...], piece[...], NT, preferred_element_type=F32
        ).astype(BF16)
        for k in range(blocks[step]):
            copy(step, k).start()
    for step in range(max(len(starts) - 2, 0), len(starts)):
        for k in range(blocks[step]):
            copy(step, k).wait()


def projection_grad(place, grad, depth, starts, pieces, before=None):
    stretch, size = grad.shape
    height = pieces[0].shape[0]
    anywhere = pl.BlockSpec(memory_space=pltpu.HBM)
    more = [] if before is None else [before]
    return pl.pallas_call(
        functools.partial(grad_proj_kernel, starts),
        in_specs=[SMEM, whole(grad)] + [whole(p) for p in pieces] + [anywhere] * len(more),
        out_specs=anywhere,
        out_shape=jax.ShapeDtypeStruct((stretch, depth), BF16),
        scratch_shapes=[pltpu.VMEM((2, stretch, height), BF16), pltpu.SemaphoreType.DMA((2, 8))],
        input_output_aliases={} if before is None else {2 + len(pieces): 0},
        compiler_params=params(),
        cost_estimate=SMALL,
        name="projection_grad",
    )(place, grad, *pieces, *more)


def grad_block_kernel(place_ref, *refs):
    sums, pick_ref, pre_ref, own_refs, other_refs = refs[:4], refs[4], refs[5], refs[6:10], refs[10:14]
    out_ref, bias_ref, pre_grad_ref = refs[14:]
    width = own_refs[0].shape[1]
    rows = own_refs[0].shape[0] // 16
    cols = sums[0].shape[0]
    total = sums[0][...].astype(F32) + sums[1][...].astype(F32)
    total = total + (sums[2][...].astype(F32) + sums[3][...].astype(F32))
    high = total.astype(BF16)
    rest = total - high.astype(F32)
    middle = rest.astype(BF16)
    low = (rest - middle.astype(F32)).astype(BF16)
    for head in range(pick_ref.shape[0]):
        own = slice(head * cols, (head + 1) * cols)
        spread = sum(
            lax.dot_general(piece, pick_ref[head], NT, preferred_element_type=F32)
            for piece in (low, middle, high)
        )
        pre = pre_ref[own]
        sigma = 1.0 / (1.0 + jnp.exp(-pre))
        pre_grad = spread * (sigma * (1.0 + pre * (1.0 - sigma)))
        bias_ref[head : head + 1, :] = jnp.sum(pre_grad.T, axis=0, keepdims=True)
        pre_grad_ref[own] = pre_grad.astype(BF16)
    grad = pre_grad_ref[...]
    for i in range(4):
        for j in range(4):
            halves = [
                jnp.dot(
                    grad,
                    hidden_block(own_refs[i], other_refs[j], i, j, zl, rows),
                    preferred_element_type=F32,
                ).astype(BF16)
                for zl in range(2)
            ]
            place = pl.multiple_of(place_ref[64 + i * 4 + j] * 2 * width, 2 * width)
            out_ref[:, pl.ds(place, 2 * width)] = jnp.concatenate(halves, axis=1)


def block_grad(place, sums, pick, pre, own, other, depth):
    heads, window, size = pick.shape
    cols = sums[0].shape[0]
    args = list(sums) + [pick, pre] + [own[i] for i in range(4)] + [other[i] for i in range(4)]
    return pl.pallas_call(
        grad_block_kernel,
        in_specs=[SMEM] + [whole(a) for a in args],
        out_shape=[
            jax.ShapeDtypeStruct((heads * cols, depth), BF16),
            jax.ShapeDtypeStruct((heads, cols), F32),
        ],
        scratch_shapes=[pltpu.VMEM((heads * cols, window), BF16)],
        compiler_params=params(),
        name="block_grad",
    )(place, *args)


def place_kernel(share, info_ref, out_ref):
    core, y, x, stretch = [info_ref[k] for k in range(4)]
    for table, which in ((OWN, core), (OTHER, 1 - core)):
        for third in range(4):
            for second in range(4):
                y_at = lax.rem(y + jnp.where(which == 0, third, second), 4)
                x_at = lax.rem(x + jnp.where(which == 0, second, third), 4)
                plane = y_at * 4 + x_at
                for zh in range(2):
                    out_ref[table[third] * 8 + second * 2 + zh] = zh * 32 + which * 16 + plane
                if table is OWN:
                    out_ref[64 + third * 4 + second] = plane
    out_ref[80] = stretch // share
    out_ref[81] = lax.rem(stretch, share)


def places(core, y, x, stretch_index, share):
    return pl.pallas_call(
        functools.partial(place_kernel, share),
        in_specs=[SMEM],
        out_specs=SMEM,
        out_shape=jax.ShapeDtypeStruct((82,), jnp.int32),
        name="places",
    )(jnp.stack([core, y, x, stretch_index]).astype(jnp.int32))


def rows_kernel(info_ref, offsets_ref, ids_ref, pick_ref, base_ref, count_ref):
    heads, window, size = pick_ref.shape
    core, zh = info_ref[0], info_ref[1]
    block = window // 4
    ids = ids_ref[...]
    valid = []
    for head in range(heads):
        later = jnp.full(ids.shape, -1, jnp.int32)
        for k in range(1, 5):
            moved = jnp.concatenate([ids[:, k:], jnp.full((1, k), -1, jnp.int32)], axis=1)
            later = jnp.where(offsets_ref[head] == k, moved, later)
        valid.append(jnp.where(later == ids, 1.0, 0.0))
    flat = jnp.concatenate(valid, axis=1)
    count_ref[0] = jnp.sum(flat).astype(jnp.int32)
    length = heads * window
    before = lax.broadcasted_iota(jnp.int32, (length, length), 0) < lax.broadcasted_iota(
        jnp.int32, (length, length), 1
    )
    rank = jnp.dot(
        jnp.broadcast_to(flat, (16, length)).astype(BF16),
        jnp.where(before, 1.0, 0.0).astype(BF16),
        preferred_element_type=F32,
    )[0:1]
    slot = jnp.where(flat > 0.0, rank, -1.0)
    lanes = lax.broadcasted_iota(jnp.int32, (window, size), 1).astype(F32)

    def chosen(row):
        column = jnp.broadcast_to(row, (LANES, window)).T[:, 0:1]
        return jnp.where(column == lanes, 1.0, 0.0)

    base = jnp.zeros((window, size), F32)
    for head in range(heads):
        own = slot[:, head * window : (head + 1) * window]
        pick = chosen(own).astype(BF16)
        for g in range(4):
            spot = jnp.where(core == g % 2, 0, 2) + g // 2
            pick_ref[head, pl.ds(pl.multiple_of(spot * block, block), block), :] = pick[
                g * block : (g + 1) * block
            ]
        earlier = jnp.full(own.shape, -1.0, F32)
        for k in range(1, 5):
            moved = jnp.concatenate([jnp.full((1, k), -1.0, F32), own[:, : window - k]], axis=1)
            earlier = jnp.where(offsets_ref[head] == k, moved, earlier)
        base = base + chosen(earlier)
    base = base.astype(BF16)
    for g in range(4):
        spot = jnp.where(core == g % 2, 0, 2) + jnp.where(zh == g // 2, 0, 1)
        base_ref[pl.ds(pl.multiple_of(spot * block, block), block), :] = base[g * block : (g + 1) * block]


def packed_rows(info, offsets, doc_ids, size):
    heads, window = offsets.shape[0], doc_ids.shape[0]
    ids = doc_ids.reshape(1, window)
    return pl.pallas_call(
        rows_kernel,
        in_specs=[SMEM, SMEM, whole(ids)],
        out_specs=[
            pl.BlockSpec((heads, window, size), lambda *_: (0, 0, 0)),
            pl.BlockSpec((window, size), lambda *_: (0, 0)),
            SMEM,
        ],
        out_shape=[
            jax.ShapeDtypeStruct((heads, window, size), BF16),
            jax.ShapeDtypeStruct((window, size), BF16),
            jax.ShapeDtypeStruct((1,), jnp.int32),
        ],
        compiler_params=params(),
        name="packed_rows",
    )(info, offsets, ids)


def shards(hidden, base_logits, doc_ids, offsets, block_weight, block_bias, projection):
    heads, depth, cols = block_weight.shape
    window = doc_ids.shape[0]
    rows, width = hidden.shape
    zh, core, y, x, zl = [lax.axis_index(a) for a in AXES]
    stretch_index = lax.axis_index(AXES)
    place = places(core, y, x, stretch_index, width // cols)
    z_shift = (zh * 2 + zl).reshape(1).astype(jnp.int32)
    no_shift = jnp.zeros((1,), jnp.int32)

    weight = block_weight.transpose(0, 2, 1).reshape(heads * cols, depth)
    proj = projection.T

    info = jnp.stack([core, zh]).astype(jnp.int32)

    def run(size, hidden, base_logits, doc_ids, offsets, proj, weight):
        plane = gather_plane(hidden, z_shift, no_shift)
        own_hidden = {0: plane, **{r: fetch(plane, 3, r) for r in (1, 3)}}
        kept, left = split_columns(zh.reshape(1), [after(base_logits, plane)])
        came = lax.ppermute(left, "zh", [(0, 1), (1, 0)])

        pick, pick_base, count = packed_rows(info, offsets, doc_ids, size)

        own_hidden[2] = fetch(plane, 3, 2)
        other_hidden = {0: swap_core(plane)}
        for r in (1, 3, 2):
            own_hidden[r] = after(own_hidden[r], pick, came, place)
            other_hidden[r] = swap_core(own_hidden[r])
        pre, packed = packed_states(place, own_hidden, other_hidden, weight, block_bias, pick)

        plane = gather_plane(packed, z_shift, no_shift)
        own = {0: plane, **{r: fetch(plane, 3, r) for r in (1, 3)}}
        other = {0: swap_core(plane)}
        kept, left = split_columns(core.reshape(1), [after(kept, plane), came])
        far = swap_core(left)
        target = target_rows(kept, far, pick_base)
        logits = add_logits(place, after(proj, target), 0, [own[0], other[0]])[0]
        half = plane.shape[0] // 2
        for r in (1, 3):
            own[r] = after(own[r], logits)
        far_own = [fetch(own[1][:half], 3, 1), fetch(own[3][half:], 3, 3)]
        for r in (1, 3):
            other[r] = swap_core(own[r])
        logits = add_logits(place, proj, 2, [own[r] for r in (1, 3)], logits)[0]
        logits = add_logits(place, proj, 5, [other[r] for r in (1, 3)], logits)[0]
        far_own = [after(v, logits) for v in far_own]
        far_other = [swap_core(v) for v in far_own]
        logits = add_logits(place, proj, 4, far_own, logits)[0]
        logits, stats = add_logits(place, proj, 7, far_other, logits, target)
        grad, loss = logits_grad(stats, logits, target, count)

        def piece(row, gates=(), add=None):
            return state_grad_piece(place, proj, row, after(grad, *gates), add)

        there = {r: piece(OTHER[r]) for r in (1, 2, 3)}
        sent = {r: swap_core(there[r]) for r in (1, 2, 3)}
        here = {r: piece(OWN[r], (), sent[r]) for r in (1, 2, 3)}
        came = {r: fetch(here[r], 3, 4 - r) for r in (1, 2, 3)}
        grad_proj = projection_grad(
            place,
            after(grad, here[1], here[2], here[3]),
            depth,
            (0, 8, 16, 24, 40, 48),
            [own[0], other[0], own[1], own[3], other[1], other[3]],
        )
        there[0] = piece(OTHER[0], (grad_proj,))
        here[0] = piece(OWN[0], (), swap_core(there[0]))
        parts = [here[0]] + [after(came[r], here[0]) for r in (1, 2, 3)]
        parts = sum_cut(no_shift, [after(p, grad_proj) for p in parts])
        moved = [fetch(parts[r], 2, 4 - r) for r in (1, 3, 2)]
        grad_proj = projection_grad(
            place,
            after(grad, parts[0]),
            depth,
            (32, 36, 56, 60),
            far_own + far_other,
            grad_proj,
        )
        parts = sum_cut(z_shift, [parts[0]] + [after(m, grad_proj) for m in moved])
        sums = [parts[0]] + [fetch(parts[r], 1, 4 - r) for r in (1, 3, 2)]
        grad_block, grad_bias = block_grad(place, sums, pick, pre, own_hidden, other_hidden, depth)
        return grad_proj, grad_block, grad_bias, loss.reshape(()), count

    args = (hidden, base_logits, doc_ids, offsets, proj, weight)
    packed_size = 384
    *result, count = run(packed_size, *args)
    grad_proj, grad_block, grad_bias, loss = lax.cond(
        count[0] <= packed_size,
        lambda done, args: done,
        lambda done, args: run(heads * window, *args)[:4],
        tuple(result),
        args,
    )
    return (
        grad_proj.T,
        grad_block.reshape(heads, cols, depth).transpose(0, 2, 1),
        grad_bias,
        loss,
    )


def solution(mesh):
    fine = Mesh(mesh.devices.reshape(2, 2, 4, 4, 2), AXES)
    return jax.shard_map(
        shards,
        mesh=fine,
        in_specs=(
            P(SEQ, VOCAB),
            P(SEQ, VOCAB),
            P(),
            P(),
            P(None, None, SEQ + VOCAB),
            P(None, SEQ + VOCAB),
            P(None, VOCAB + SEQ),
        ),
        out_specs=(
            P(None, VOCAB + SEQ),
            P(None, None, SEQ + VOCAB),
            P(None, SEQ + VOCAB),
            P(),
        ),
        check_vma=False,
    )
```
